1024 devices in a mesh: dp: 16 (over y, z_lo), mp: 64 (over x, z_hi, core).
Axes of the slice: x: 8, y: 8, z: 8 (z_hi: 4, z_lo: 2; z = z_hi * 2 + z_lo), core: 2. Of those that a mesh axis runs over, the one named last changes fastest.
Arguments:
- tokens: bfloat16 [4096, 4096], P('dp'), may hold values from -96 to 96
- inner_weight: float32 [2, 4096, 16384], P(None, 'dp', 'mp'), may hold values from -5 to 5, as said below
- inner_grad: float32 [2, 4096, 16384], P(None, 'dp', 'mp'), may hold values from -400 to 400
- inner_row: float32 [2, 4096], P(None, 'dp'), may hold values from 0.01 to 1
- inner_col: float32 [2, 16384], P(None, 'mp'), may hold values from 0.01 to 1
- outer_weight: float32 [16384, 4096], P('mp', 'dp'), may hold values from -5 to 5, as said below
- outer_grad: float32 [16384, 4096], P('mp', 'dp'), may hold values from -400 to 400
- outer_row: float32 [16384], P('mp'), may hold values from 0.01 to 1
- outer_col: float32 [4096], P('dp'), may hold values from 0.01 to 1
Outputs:
- inner_new: float32 [2, 4096, 16384], P(None, 'dp', 'mp')
- inner_update: float32 [2, 4096, 16384], P(None, 'dp', 'mp')
- inner_row_new: float32 [2, 4096], P(None, 'dp')
- inner_col_new: float32 [2, 16384], P(None, 'mp')
- outer_new: float32 [16384, 4096], P('mp', 'dp')
- outer_update: float32 [16384, 4096], P('mp', 'dp')
- outer_row_new: float32 [16384], P('mp')
- outer_col_new: float32 [4096], P('dp')
- hidden: bfloat16 [4096, 16384], P('dp', 'mp')
The draws below stay inside these ranges and needn't reach their ends.
Inputs may be any that keep to these rules, and one draw needn't show every extreme that they name: `inner_weight`: parameters of the gate and up projections. `outer_weight`: parameters of the down projection.
All inputs are finite; a program needn't handle non-finite values.
Results may differ from the reference program's by a relative error of at most 0.0058.
Values may be sent and summed in bfloat16 or wider, within the bound.
A program may use at most 32 MiB of HBM per device.

```python
import math
import jax
import jax.numpy as jnp
from jax import lax

D = 4096
FF = 16384
STEP = 10
TOKENS = 4096


def scaled_field(key, leading, row_count, col_count):
    subkeys = jax.random.split(key, 3)
    row_scale = jnp.exp(jax.random.uniform(subkeys[0], (leading, row_count, 1), jnp.float32, math.log(0.3), math.log(3.0)))
    col_scale = jnp.exp(jax.random.uniform(subkeys[1], (leading, 1, col_count), jnp.float32, math.log(0.3), math.log(3.0)))
    row_ramp = 1.0 + 2.0 * jnp.arange(row_count, dtype=jnp.float32)[None, :, None] / (row_count - 1)
    col_ramp = 1.0 + 2.0 * jnp.arange(col_count, dtype=jnp.float32)[None, None, :] / (col_count - 1)
    pattern = jnp.clip(jax.random.normal(subkeys[2], (leading, row_count, col_count), jnp.float32), -4.0, 4.0)
    return pattern * row_scale * col_scale * row_ramp * col_ramp


def weight_field(key, leading, row_count, col_count, fan_in):
    subkeys = jax.random.split(key, 3)
    row_scale = jnp.exp(jax.random.uniform(subkeys[0], (leading, row_count, 1), jnp.float32, math.log(0.3), math.log(3.0)))
    col_scale = jnp.exp(jax.random.uniform(subkeys[1], (leading, 1, col_count), jnp.float32, math.log(0.3), math.log(3.0)))
    row_ramp = 1.0 + 0.732 * jnp.arange(row_count, dtype=jnp.float32)[None, :, None] / (row_count - 1)
    col_ramp = 1.0 + 0.732 * jnp.arange(col_count, dtype=jnp.float32)[None, None, :] / (col_count - 1)
    pattern = jnp.clip(jax.random.normal(subkeys[2], (leading, row_count, col_count), jnp.float32), -4.0, 4.0)
    return pattern * row_scale * col_scale * row_ramp * col_ramp * (0.3 / math.sqrt(fan_in))


def draw_tokens(key, part):
    base_key = jax.random.fold_in(key, 43)
    base = jnp.clip(jax.random.normal(base_key, (TOKENS, D), jnp.float32), -6.0, 6.0)
    feature_gain = jnp.where(jnp.arange(D) < D // 4, 16.0, 1.0).astype(jnp.float32)
    return (base * feature_gain[None, :]).astype(jnp.bfloat16)


def draw_inner_grad(key, part):
    field = scaled_field(jax.random.fold_in(key, 11), 2, D, FF)
    subkeys = jax.random.split(jax.random.fold_in(key, 13), 2)
    row_flag = jax.random.randint(subkeys[0], (D, 1), 0, 2).astype(jnp.float32)
    col_flag = jax.random.randint(subkeys[1], (1, FF), 0, 2).astype(jnp.float32)
    interplay = 0.1 + 0.9 * row_flag * col_flag
    gate_grad = field[0] * interplay
    up_grad = field[1] * 0.002
    return jnp.stack([gate_grad, up_grad], axis=0)


def draw_outer_grad(key, part):
    return scaled_field(jax.random.fold_in(key, 23), 1, FF, D)[0]


def draw_inner_weight(key, part):
    field = weight_field(jax.random.fold_in(key, 31), 2, D, FF, D)
    row_gain = jnp.where(jnp.arange(D) < D // 4, 0.01, 1.0).astype(jnp.float32)
    return field * row_gain[None, :, None]


def draw_outer_weight(key, part):
    return weight_field(jax.random.fold_in(key, 37), 1, FF, D, FF)[0]


def levels(rng, dims, cuts, smallest, top_value):
    gain, own = 1.0, jax.random.fold_in(rng, 6)
    for position, blocks in cuts:
        steps = jnp.exp(jax.random.uniform(jax.random.fold_in(own, position), (blocks,), jnp.float32, smallest / len(cuts), top_value / len(cuts)))
        gain = gain * jnp.repeat(steps, dims[position] // blocks).reshape([-1 if axis == position else 1 for axis in range(len(dims))])
    return gain


def setup_inputs(seed: int = 0) -> dict:
    splits = jax.random.split(jax.random.key(seed), 10)
    tokens = draw_tokens(jax.random.fold_in(splits[9], 71), 0)
    inner_weight = draw_inner_weight(jax.random.fold_in(splits[9], 71), 0)
    inner_grad = draw_inner_grad(jax.random.fold_in(splits[9], 71), 0)
    inner_row = jnp.clip(jnp.exp(math.log(1.0) - 4.6051702 * jax.random.uniform(splits[3], (2, D), jnp.float32) ** levels(splits[3], (2, D), ((1, 16),), -0.2, 0.2)), 0.01, 1.0)
    inner_col = jnp.clip(jnp.exp(math.log(1.0) - 4.6051702 * jax.random.uniform(splits[4], (2, FF), jnp.float32) ** levels(splits[4], (2, FF), ((1, 64),), -0.2, 0.2)), 0.01, 1.0)
    outer_weight = draw_outer_weight(jax.random.fold_in(splits[9], 71), 0)
    outer_grad = draw_outer_grad(jax.random.fold_in(splits[9], 71), 0)
    outer_row = jnp.clip(jnp.exp(math.log(1.0) - 4.6051702 * jax.random.uniform(splits[7], (FF,), jnp.float32) ** levels(splits[7], (FF,), ((0, 64),), -0.2, 0.2)), 0.01, 1.0)
    outer_col = jnp.clip(jnp.exp(math.log(1.0) - 4.6051702 * jax.random.uniform(splits[8], (D,), jnp.float32) ** levels(splits[8], (D,), ((0, 16),), -0.2, 0.2)), 0.01, 1.0)
    return {"tokens": tokens, "inner_weight": inner_weight, "inner_grad": inner_grad, "inner_row": inner_row, "inner_col": inner_col, "outer_weight": outer_weight, "outer_grad": outer_grad, "outer_row": outer_row, "outer_col": outer_col}


def factor_update(param, grad, row, col):
    forget = 1.0 - STEP ** (-0.8)
    relative = min(0.01, STEP ** (-0.5))
    square = grad * grad + 1e-30
    row_new = forget * row + (1.0 - forget) * lax.optimization_barrier(jnp.mean(square, axis=-1))
    col_new = forget * col + (1.0 - forget) * lax.optimization_barrier(jnp.mean(square, axis=-2))
    row_mean = lax.optimization_barrier(jnp.mean(row_new, axis=-1))
    vhat = row_new[..., :, None] * col_new[..., None, :] / row_mean[..., None, None]
    raw = grad / jnp.sqrt(vhat)
    clip_factor = jnp.maximum(1.0, jnp.sqrt(lax.optimization_barrier(jnp.mean(raw * raw, axis=(-2, -1)))))
    step_size = relative * jnp.sqrt(lax.optimization_barrier(jnp.mean(param * param, axis=(-2, -1))))
    update = -(step_size / clip_factor)[..., None, None] * raw
    updated = param + update
    return (updated, update, row_new, col_new)

def reference(tokens, inner_weight, inner_grad, inner_row, inner_col, outer_weight, outer_grad, outer_row, outer_col):
    inner_new, inner_update, inner_row_new, inner_col_new = factor_update(inner_weight, inner_grad, inner_row, inner_col)
    outer_new, outer_update, outer_row_new, outer_col_new = factor_update(outer_weight, outer_grad, outer_row, outer_col)
    inner_cast = inner_new.astype(jnp.bfloat16)
    gate_pre = jnp.dot(tokens, inner_cast[0], preferred_element_type=jnp.float32)
    up_pre = jnp.dot(tokens, inner_cast[1], preferred_element_type=jnp.float32)
    hidden = (jax.nn.gelu(gate_pre, approximate=True) * up_pre).astype(jnp.bfloat16)
    return (inner_new, inner_update, inner_row_new, inner_col_new, outer_new, outer_update, outer_row_new, outer_col_new, hidden)
```

```python
import functools

import jax
import jax.numpy as jnp
from jax import lax
from jax.experimental import pallas as pl
from jax.experimental.pallas import tpu as pltpu
from jax.sharding import PartitionSpec as P

D = 4096
FF = 16384
STEP = 10
FORGET = 1.0 - STEP ** (-0.8)
FRESH = 1.0 - FORGET
RELATIVE = min(0.01, STEP ** (-0.5))

NY = 8
B = 256
H = 128
CHUNKS = 4
C64 = 64
MESH = pl.DeviceIdType.MESH


def rows_to_lanes(q):
    return jnp.sum((q[:, :H] + q[:, H:]).T, axis=0, keepdims=True)


def lanes_to_rows(v):
    return jnp.concatenate(
        [jnp.broadcast_to(v[:, :H], (H, H)).T, jnp.broadcast_to(v[:, H:], (H, H)).T], axis=0
    )


def kernel(
    tok, iw, ig, irow, icol, ow, og, orow, ocol,
    inew, iupd, irow_new, icol_new, onew, oupd, orow_new, ocol_new, hid,
    g_v, w_v, raw, new_v, upd_v, tokbuf, agbuf, acc, zbuf, hid_v,
    dp1, mx, mz, dp2, snd, scal,
    load_sem, tok_sem, out_sem, st_send, st_recv, tx_send, tx_recv, sib_send, sib_recv,
    ag_send, ag_recv, z_send, z_recv,
):
    dp, mp = lax.axis_index("dp"), lax.axis_index("mp")
    y, z = dp // 2, lax.rem(dp, 2)
    x, zc = mp // 8, lax.rem(mp, 8)
    core = lax.rem(mp, 2)

    def dp_peer(k):
        return (lax.rem(dp + k, 16), mp)

    def x_peer(k):
        return (dp, lax.rem(x + k, 8) * 8 + zc)

    def zc_peer(k):
        return (dp, x * 8 + lax.rem(zc + k, 8))

    y_next = (lax.rem(y + 1, NY) * 2 + z, mp)
    y_prev = (lax.rem(y + NY - 1, NY) * 2 + z, mp)
    z_pair = (y * 2 + 1 - z, mp)
    sibling = (dp, mp + 1 - 2 * core)

    barrier = pltpu.get_barrier_semaphore()
    for k in range(1, 16):
        pl.semaphore_signal(barrier, inc=1, device_id=dp_peer(k), device_id_type=MESH)
    for k in range(1, 8):
        pl.semaphore_signal(barrier, inc=1, device_id=x_peer(k), device_id_type=MESH)
        pl.semaphore_signal(barrier, inc=1, device_id=zc_peer(k), device_id_type=MESH)

    loads = [
        pltpu.make_async_copy(ig, g_v.at[pl.ds(0, 2)], load_sem.at[0]),
        pltpu.make_async_copy(og, g_v.at[2], load_sem.at[1]),
        pltpu.make_async_copy(iw, w_v.at[pl.ds(0, 2)], load_sem.at[2]),
        pltpu.make_async_copy(ow, w_v.at[2], load_sem.at[3]),
    ]
    for c in loads:
        c.start()
    own_tok = []
    for b in range(NY):
        c = pltpu.make_async_copy(
            tok.at[:, pl.ds(pl.multiple_of((2 * b + z) * B, B), B)],
            tokbuf.at[b, pl.ds(0, B), :],
            tok_sem.at[b],
        )
        c.start()
        own_tok.append(c)

    loads[0].wait()
    for k in range(2):
        g = g_v[k]
        v = jnp.sum(g * g + 1e-30, axis=0, keepdims=True)
        snd[0, 2 * k : 2 * k + 1, :] = v[:, :H]
        snd[0, 2 * k + 1 : 2 * k + 2, :] = v[:, H:]
    loads[1].wait()
    g = g_v[2]
    v = rows_to_lanes(g * g + 1e-30)
    snd[0, 4:5, :] = v[:, :H]
    snd[0, 5:6, :] = v[:, H:]
    snd[0, 6:8, :] = jnp.zeros((2, H), jnp.float32)

    pl.semaphore_wait(barrier, 29)

    def exchange(slot, me, peers, src, row0, stage):
        rows = slot.shape[1]
        for p in peers:
            pltpu.make_async_remote_copy(
                src_ref=src, dst_ref=slot.at[me], send_sem=st_send.at[stage], recv_sem=st_recv.at[stage],
                device_id=p, device_id_type=MESH,
            ).start()

    def arrived(slot, stage, n):
        part = slot.at[pl.ds(0, n)]
        pltpu.make_async_copy(part, part, st_recv.at[stage]).wait()

    def sent(slot, stage, n):
        part = slot.at[pl.ds(0, n)]
        pltpu.make_async_copy(part, part, st_send.at[stage]).wait()

    exchange(dp1, dp, [dp_peer(k) for k in range(1, 16)], snd.at[0, pl.ds(0, 8)], 0, 0)
    dp1[dp] = snd[0, 0:8, :]

    tok_out = []
    for j in range(4):
        b = core * 4 + j
        c = pltpu.make_async_remote_copy(
            src_ref=tok.at[:, pl.ds(pl.multiple_of((2 * b + 1 - z) * B, B), B)],
            dst_ref=tokbuf.at[b, pl.ds(B, B), :],
            send_sem=tx_send.at[j], recv_sem=tx_recv.at[j],
            device_id=z_pair, device_id_type=MESH,
        )
        c.start()
        tok_out.append(c)

    for k in range(2):
        g = g_v[k]
        v = rows_to_lanes(g * g + 1e-30)
        snd[1, 2 * k : 2 * k + 1, :] = v[:, :H]
        snd[1, 2 * k + 1 : 2 * k + 2, :] = v[:, H:]
    g = g_v[2]
    v = jnp.sum(g * g + 1e-30, axis=0, keepdims=True)
    snd[1, 4:5, :] = v[:, :H]
    snd[1, 5:6, :] = v[:, H:]
    loads[2].wait()
    loads[3].wait()
    for k in range(3):
        w = w_v[k]
        v = jnp.sum(w * w, axis=0, keepdims=True)
        snd[1, 12 + k : 13 + k, :] = v[:, :H] + v[:, H:]

    arrived(dp1, 0, 15)
    tot = dp1[0]
    for i in range(1, 16):
        tot = tot + dp1[i]
    scal[0:8, :] = tot

    old = [icol[0:1, :], icol[1:2, :], orow[...]]
    fc = []
    for k in range(3):
        s = jnp.concatenate([scal[2 * k : 2 * k + 1, :], scal[2 * k + 1 : 2 * k + 2, :]], axis=1)
        fc.append(FORGET * old[k] + FRESH * (s / D))
    icol_new[0:1, :] = fc[0]
    icol_new[1:2, :] = fc[1]
    orow_new[...] = fc[2]
    snd[1, 15:16, :] = fc[2][:, :H] + fc[2][:, H:]
    for k in range(2):
        g = g_v[k]
        v = rows_to_lanes(g * g * (1.0 / fc[k]))
        snd[1, 6 + 2 * k : 7 + 2 * k, :] = v[:, :H]
        snd[1, 7 + 2 * k : 8 + 2 * k, :] = v[:, H:]
    g = g_v[2]
    c2 = lanes_to_rows(lax.rsqrt(fc[2]))
    c2 = jnp.concatenate([c2, c2], axis=1)
    gs = g * c2
    v = jnp.sum(gs * gs, axis=0, keepdims=True)
    snd[1, 10:11, :] = v[:, :H]
    snd[1, 11:12, :] = v[:, H:]
    raw[2] = gs

    exchange(mx, x, [x_peer(k) for k in range(1, 8)], snd.at[1], 0, 1)
    mx[x] = snd[1]
    for k in range(2):
        raw[k] = g_v[k] * lax.rsqrt(fc[k])
    arrived(mx, 1, 7)
    tot = mx[0]
    for i in range(1, 8):
        tot = tot + mx[i]
    snd[2] = tot
    exchange(mz, zc, [zc_peer(k) for k in range(1, 8)], snd.at[2], 0, 2)
    mz[zc] = snd[2]
    sib_out = []
    for j in range(4):
        b = core * 4 + j
        tok_out[j].wait_recv()
        c = pltpu.make_async_remote_copy(
            src_ref=tokbuf.at[b, pl.ds(B, B), :],
            dst_ref=tokbuf.at[b, pl.ds(B, B), :],
            send_sem=sib_send.at[j], recv_sem=sib_recv.at[j],
            device_id=sibling, device_id_type=MESH,
        )
        c.start()
        sib_out.append(c)
    arrived(mz, 2, 7)
    tot = mz[0]
    for i in range(1, 8):
        tot = tot + mz[i]
    scal[16:32, :] = tot

    old = [irow[0:1, :], irow[1:2, :], ocol[...]]
    fr = []
    for k in range(3):
        r = 16 + 2 * k
        s = jnp.concatenate([scal[r : r + 1, :], scal[r + 1 : r + 2, :]], axis=1)
        f = FORGET * old[k] + FRESH * (s / FF)
        fr.append(f)
        r = 22 + 2 * k
        t = jnp.concatenate([scal[r : r + 1, :], scal[r + 1 : r + 2, :]], axis=1)
        u = t / f
        snd[3, k : k + 1, :] = u[:, :H] + u[:, H:]
        snd[3, 3 + k : 4 + k, :] = scal[28 + k : 29 + k, :]
    irow_new[0:1, :] = fr[0]
    irow_new[1:2, :] = fr[1]
    ocol_new[...] = fr[2]
    for k in range(2):
        snd[3, 6 + k : 7 + k, :] = fr[k][:, :H] + fr[k][:, H:]
    exchange(dp2, dp, [dp_peer(k) for k in range(1, 16)], snd.at[3, pl.ds(0, 8)], 0, 3)
    dp2[dp] = snd[3, 0:8, :]

    for k in range(2):
        rr = lanes_to_rows(lax.rsqrt(fr[k]))
        raw[k] = raw[k] * jnp.concatenate([rr, rr], axis=1)
    raw[2] = raw[2] * lax.rsqrt(fr[2])
    mean2 = jnp.sum(scal[31:32, :], axis=1, keepdims=True) / FF

    arrived(dp2, 3, 15)
    tot = dp2[0]
    for i in range(1, 16):
        tot = tot + dp2[i]
    scal[0:8, :] = jnp.broadcast_to(jnp.sum(tot, axis=1, keepdims=True), (8, H))

    coef = []
    for k in range(3):
        mean = scal[6 + k : 7 + k, 0:1] / D if k < 2 else mean2
        clip = jnp.maximum(1.0, jnp.sqrt(scal[k : k + 1, 0:1] * mean / (D * FF)))
        step = RELATIVE * jnp.sqrt(scal[3 + k : 4 + k, 0:1] / (D * FF))
        coef.append(step / clip * jnp.sqrt(mean))

    for k in range(2):
        u = raw[k] * (-coef[k])
        upd_v[k] = u
        new_v[k] = w_v[k] + u

    def ag_copy(way, c, s):
        src = lax.rem(y + NY - (s - 1), NY) if way == 0 else lax.rem(y + s - 1, NY)
        return pltpu.make_async_remote_copy(
            src_ref=agbuf.at[c, src], dst_ref=agbuf.at[c, src],
            send_sem=ag_send.at[way, c, s - 1], recv_sem=ag_recv.at[way, c, s - 1],
            device_id=y_next if way == 0 else y_prev, device_id_type=MESH,
        )

    def steps(way, c):
        return 4 if (c % 2 == 0) == (way == 0) else 3

    for c in range(CHUNKS):
        lo = c * C64
        block = jnp.concatenate([new_v[0, :, lo : lo + C64], new_v[1, :, lo : lo + C64]], axis=1)
        agbuf[c, y] = block.astype(jnp.bfloat16)
        for way in range(2):
            ag_copy(way, c, 1).start()

    u = raw[2] * (-coef[2])
    upd_v[2] = u
    new_v[2] = w_v[2] + u
    outs = [
        pltpu.make_async_copy(new_v.at[pl.ds(0, 2)], inew, out_sem.at[0]),
        pltpu.make_async_copy(upd_v.at[pl.ds(0, 2)], iupd, out_sem.at[1]),
        pltpu.make_async_copy(new_v.at[2], onew, out_sem.at[2]),
        pltpu.make_async_copy(upd_v.at[2], oupd, out_sem.at[3]),
    ]
    for c in outs:
        c.start()

    for c in own_tok:
        c.wait()
    for c in sib_out:
        c.wait()

    def product(c, b, first):
        part = jnp.dot(tokbuf[b], agbuf[c, b], preferred_element_type=jnp.float32)
        if first:
            acc[c] = part
        else:
            acc[c] += part

    for c in range(CHUNKS):
        product(c, y, True)

    z_out = [
        pltpu.make_async_remote_copy(
            src_ref=acc.at[c, pl.ds(B, B), :], dst_ref=zbuf.at[c],
            send_sem=z_send.at[c], recv_sem=z_recv.at[c],
            device_id=z_pair, device_id_type=MESH,
        )
        for c in range(CHUNKS)
    ]
    for s in range(1, 5):
        for c in range(CHUNKS):
            for way in range(2):
                if s > steps(way, c):
                    continue
                ag_copy(way, c, s).wait_recv()
                if s < steps(way, c):
                    ag_copy(way, c, s + 1).start()
                b = lax.rem(y + NY - s, NY) if way == 0 else lax.rem(y + s, NY)
                product(c, b, False)
            if s == 4:
                z_out[c].start()

    lane = lax.broadcasted_iota(jnp.int32, (B, H), 1)
    hid_out = []
    for p in range(CHUNKS // 2):
        both = []
        for c in (2 * p, 2 * p + 1):
            z_out[c].wait_recv()
            both.append(acc[c, 0:B, :] + zbuf[c])
        left, right = both
        gate = jnp.where(lane < C64, left, pltpu.roll(right, C64, 1))
        up = jnp.where(lane < C64, pltpu.roll(left, C64, 1), right)
        hid_v[p] = (jax.nn.gelu(gate, approximate=True) * up).astype(jnp.bfloat16)
        c = pltpu.make_async_copy(hid_v.at[p], hid.at[:, pl.ds(p * H, H)], out_sem.at[4 + p])
        c.start()
        hid_out.append(c)

    sent(dp1, 0, 15)
    sent(mx, 1, 7)
    sent(mz, 2, 7)
    sent(dp2, 3, 15)
    for c in tok_out:
        c.wait_send()
    for c in range(CHUNKS):
        for way in range(2):
            for s in range(1, steps(way, c) + 1):
                ag_copy(way, c, s).wait_send()
        z_out[c].wait_send()
    for c in outs:
        c.wait()
    for c in hid_out:
        c.wait()


def per_device(tokens, iw, ig, irow, icol, ow, og, orow, ocol):
    f32, bf16 = jnp.float32, jnp.bfloat16
    hbm = pl.BlockSpec(memory_space=pl.ANY)
    vm = pl.BlockSpec(memory_space=pltpu.VMEM)
    sds = jax.ShapeDtypeStruct
    outs = pl.pallas_call(
        kernel,
        out_shape=(
            sds((2, B, B), f32), sds((2, B, B), f32), sds((2, B), f32), sds((2, B), f32),
            sds((B, B), f32), sds((B, B), f32), sds((1, B), f32), sds((1, B), f32), sds((B, B), bf16),
        ),
        in_specs=[hbm, hbm, hbm, vm, vm, hbm, hbm, vm, vm],
        out_specs=(hbm, hbm, vm, vm, hbm, hbm, vm, vm, hbm),
        scratch_shapes=[
            pltpu.VMEM((3, B, B), f32),
            pltpu.VMEM((3, B, B), f32),
            pltpu.VMEM((3, B, B), f32),
            pltpu.VMEM((3, B, B), f32),
            pltpu.VMEM((3, B, B), f32),
            pltpu.VMEM((NY, 2 * B, B), bf16),
            pltpu.VMEM((CHUNKS, NY, B, H), bf16),
            pltpu.VMEM((CHUNKS, 2 * B, H), f32),
            pltpu.VMEM((CHUNKS, B, H), f32),
            pltpu.VMEM((CHUNKS // 2, B, H), bf16),
            pltpu.VMEM((16, 8, H), f32),
            pltpu.VMEM((8, 16, H), f32),
            pltpu.VMEM((8, 16, H), f32),
            pltpu.VMEM((16, 8, H), f32),
            pltpu.VMEM((4, 16, H), f32),
            pltpu.VMEM((32, H), f32),
            pltpu.SemaphoreType.DMA((4,)),
            pltpu.SemaphoreType.DMA((NY,)),
            pltpu.SemaphoreType.DMA((6,)),
            pltpu.SemaphoreType.DMA((4,)),
            pltpu.SemaphoreType.DMA((4,)),
            pltpu.SemaphoreType.DMA((4,)),
            pltpu.SemaphoreType.DMA((4,)),
            pltpu.SemaphoreType.DMA((4,)),
            pltpu.SemaphoreType.DMA((4,)),
            pltpu.SemaphoreType.DMA((2, CHUNKS, 4)),
            pltpu.SemaphoreType.DMA((2, CHUNKS, 4)),
            pltpu.SemaphoreType.DMA((CHUNKS,)),
            pltpu.SemaphoreType.DMA((CHUNKS,)),
        ],
        compiler_params=pltpu.CompilerParams(
            collective_id=0, has_side_effects=True, vmem_limit_bytes=40 * 1024 * 1024
        ),
        cost_estimate=pl.CostEstimate(
            flops=2 * B * D * 2 * B, bytes_accessed=5 * 1024 * 1024, transcendentals=B * B
        ),
    )(tokens, iw, ig, irow, icol, ow, og, orow.reshape(1, B), ocol.reshape(1, B))
    outs = list(outs)
    outs[6] = outs[6].reshape(B)
    outs[7] = outs[7].reshape(B)
    return tuple(outs)


def solution(mesh):
    placed = (
        P("dp", None),
        P(None, "dp", "mp"),
        P(None, "dp", "mp"),
        P(None, "dp"),
        P(None, "mp"),
        P("mp", "dp"),
        P("mp", "dp"),
        P("mp"),
        P("dp"),
    )
    return jax.shard_map(
        per_device,
        mesh=mesh,
        in_specs=placed,
        out_specs=(
            P(None, "dp", "mp"),
            P(None, "dp", "mp"),
            P(None, "dp"),
            P(None, "mp"),
            P("mp", "dp"),
            P("mp", "dp"),
            P("mp"),
            P("dp"),
            P("dp", "mp"),
        ),
        check_vma=False,
    )
```

```python
import functools

import jax
import jax.numpy as jnp
from jax import lax
from jax.experimental import pallas as pl
from jax.experimental.pallas import tpu as pltpu
from jax.sharding import PartitionSpec as P

D = 4096
FF = 16384
STEP = 10
FORGET = 1.0 - STEP ** (-0.8)
FRESH = 1.0 - FORGET
RELATIVE = min(0.01, STEP ** (-0.5))

NY = 8
B = 256
H = 128
CHUNKS = 4
EARLY = 2
STREAMS = 2 * EARLY + CHUNKS - EARLY
C64 = 64
MESH = pl.DeviceIdType.MESH


def rows_to_lanes(q):
    return jnp.sum((q[:, :H] + q[:, H:]).T, axis=0, keepdims=True)


def lanes_to_rows(v):
    return jnp.concatenate(
        [jnp.broadcast_to(v[:, :H], (H, H)).T, jnp.broadcast_to(v[:, H:], (H, H)).T], axis=0
    )


def far_first(n):
    return sorted(range(1, n), key=lambda k: -min(k, n - k))


def kernel(
    tok, iw, ig, irow, icol, ow, og, orow, ocol,
    inew, iupd, irow_new, icol_new, onew, oupd, orow_new, ocol_new, hid,
    g_v, w_v, raw, new_v, upd_v, tokbuf, agbuf, acc, zbuf, zout_v, zin_v, hid_v,
    dp1, rx, rz, tx, tz, dp2, snd, scal, rmat,
    load_sem, tok_sem, out_sem, st_send, st_recv, tx_send, tx_recv, sib_send, sib_recv,
    ag_send, ag_recv, z_send, z_recv,
):
    dp, mp = lax.axis_index("dp"), lax.axis_index("mp")
    y, z = dp // 2, lax.rem(dp, 2)
    x, zc = mp // 8, lax.rem(mp, 8)
    core = lax.rem(mp, 2)

    dp_peers = [(lax.rem(dp + k, 16), mp) for k in far_first(16)]
    x_peers = [(dp, lax.rem(x + k, 8) * 8 + zc) for k in far_first(8)]
    zc_peers = [(dp, x * 8 + lax.rem(zc + k, 8)) for k in far_first(8)]
    y_next = (lax.rem(y + 1, NY) * 2 + z, mp)
    y_prev = (lax.rem(y + NY - 1, NY) * 2 + z, mp)
    z_pair = (y * 2 + 1 - z, mp)
    sibling = (dp, mp + 1 - 2 * core)

    barrier = pltpu.get_barrier_semaphore()
    for peer in dp_peers + x_peers + zc_peers:
        pl.semaphore_signal(barrier, inc=1, device_id=peer, device_id_type=MESH)

    loads = [
        pltpu.make_async_copy(ig, g_v.at[pl.ds(0, 2)], load_sem.at[0]),
        pltpu.make_async_copy(og, g_v.at[2], load_sem.at[1]),
        pltpu.make_async_copy(iw, w_v.at[pl.ds(0, 2)], load_sem.at[2]),
        pltpu.make_async_copy(ow, w_v.at[2], load_sem.at[3]),
    ]
    for c in loads:
        c.start()
    own_tok = []
    for b in range(NY):
        c = pltpu.make_async_copy(
            tok.at[:, pl.ds(pl.multiple_of((2 * b + z) * B, B), B)],
            tokbuf.at[b, pl.ds(0, B), :],
            tok_sem.at[b],
        )
        c.start()
        own_tok.append(c)

    def put(i, row, v):
        snd[i, row : row + 1, :] = v[:, :H]
        snd[i, row + 1 : row + 2, :] = v[:, H:]

    def take(row):
        return jnp.concatenate([scal[row : row + 1, :], scal[row + 1 : row + 2, :]], axis=1)

    def exchange(slot, me, peers, src, stage):
        for p in peers:
            pltpu.make_async_remote_copy(
                src_ref=src, dst_ref=slot.at[me], send_sem=st_send.at[stage], recv_sem=st_recv.at[stage],
                device_id=p, device_id_type=MESH,
            ).start()
        slot[me] = src[...]

    def arrived(slot, stage):
        n = slot.shape[0]
        part = slot.at[pl.ds(0, n - 1)]
        pltpu.make_async_copy(part, part, st_recv.at[stage]).wait()
        tot = slot[0]
        for i in range(1, n):
            tot = tot + slot[i]
        return tot

    def sent(slot, stage):
        part = slot.at[pl.ds(0, slot.shape[0] - 1)]
        pltpu.make_async_copy(part, part, st_send.at[stage]).wait()

    def ag_copy(way, st, s):
        src = lax.rem(y + NY - (s - 1), NY) if way == 0 else lax.rem(y + s - 1, NY)
        return pltpu.make_async_remote_copy(
            src_ref=agbuf.at[st, src], dst_ref=agbuf.at[st, src],
            send_sem=ag_send.at[way, st, s - 1], recv_sem=ag_recv.at[way, st, s - 1],
            device_id=y_next if way == 0 else y_prev, device_id_type=MESH,
        )

    def steps(way, st):
        return 4 if (st % 2 == 0) == (way == 0) else 3

    def origin(way, s):
        return lax.rem(y + NY - s, NY) if way == 0 else lax.rem(y + s, NY)

    def launch(st, pair, c):
        lo = c * C64
        block = jnp.concatenate([pair[0, :, lo : lo + C64], pair[1, :, lo : lo + C64]], axis=1)
        agbuf[st, y] = block.astype(jnp.bfloat16)
        for way in range(2):
            ag_copy(way, st, 1).start()

    def relay(st, s):
        for way in range(2):
            if s <= steps(way, st):
                ag_copy(way, st, s).wait_recv()
                if s < steps(way, st):
                    ag_copy(way, st, s + 1).start()

    def product(st, b, first=False):
        part = jnp.dot(tokbuf[b], agbuf[st, b], preferred_element_type=jnp.float32)
        if first:
            acc[st] = part
        else:
            acc[st] += part

    def products(st, s):
        for way in range(2):
            if s <= steps(way, st):
                product(st, origin(way, s))

    snd[...] = jnp.zeros_like(snd)
    loads[0].wait()
    for k in range(2):
        g = g_v[k]
        put(0, 2 * k, jnp.sum(g * g + 1e-30, axis=0, keepdims=True))
    loads[1].wait()
    g = g_v[2]
    put(0, 4, rows_to_lanes(g * g + 1e-30))

    pl.semaphore_wait(barrier, 29)
    exchange(dp1, dp, dp_peers, snd.at[0], 0)

    loads[2].wait()
    for c in range(EARLY):
        launch(c, w_v, c)
    for c in range(EARLY):
        launch(EARLY + c, g_v, c)

    tok_out = []
    for j in range(4):
        b = core * 4 + j
        c = pltpu.make_async_remote_copy(
            src_ref=tok.at[:, pl.ds(pl.multiple_of((2 * b + 1 - z) * B, B), B)],
            dst_ref=tokbuf.at[b, pl.ds(B, B), :],
            send_sem=tx_send.at[j], recv_sem=tx_recv.at[j],
            device_id=z_pair, device_id_type=MESH,
        )
        c.start()
        tok_out.append(c)

    for k in range(2):
        g = g_v[k]
        put(1, 2 * k, rows_to_lanes(g * g + 1e-30))
    g = g_v[2]
    put(1, 4, jnp.sum(g * g + 1e-30, axis=0, keepdims=True))
    exchange(rx, x, x_peers, snd.at[1], 1)
    loads[3].wait()
    lane1 = lax.broadcasted_iota(jnp.int32, (1, H), 1)
    misc = jnp.zeros((1, H), jnp.float32)
    for k in range(3):
        w = w_v[k]
        v = jnp.sum(w * w, axis=0, keepdims=True)
        misc = jnp.where(lane1 == k, jnp.sum(v, axis=1, keepdims=True), misc)

    scal[0:8, :] = arrived(dp1, 0)
    old = [icol[0:1, :], icol[1:2, :], orow[...]]
    fc = [FORGET * old[k] + FRESH * (take(2 * k) / D) for k in range(3)]
    cc = [lax.rsqrt(f) for f in fc]
    misc = jnp.where(lane1 == 3, jnp.sum(fc[2], axis=1, keepdims=True), misc)
    snd[2, 6:7, :] = misc
    for k in range(2):
        g = g_v[k] * cc[k]
        raw[k] = g
        put(2, 2 * k, rows_to_lanes(g * g))
    c2 = lanes_to_rows(cc[2])
    g = g_v[2] * jnp.concatenate([c2, c2], axis=1)
    raw[2] = g
    put(2, 4, jnp.sum(g * g, axis=0, keepdims=True))
    exchange(tx, x, x_peers, snd.at[2], 2)
    icol_new[0:1, :] = fc[0]
    icol_new[1:2, :] = fc[1]
    orow_new[...] = fc[2]

    snd[3] = arrived(rx, 1)
    exchange(rz, zc, zc_peers, snd.at[3], 3)
    for st in range(2 * EARLY):
        relay(st, 1)
    snd[4] = arrived(tx, 2)
    exchange(tz, zc, zc_peers, snd.at[4], 4)

    sib_out = []
    for j in range(4):
        b = core * 4 + j
        tok_out[j].wait_recv()
        c = pltpu.make_async_remote_copy(
            src_ref=tokbuf.at[b, pl.ds(B, B), :],
            dst_ref=tokbuf.at[b, pl.ds(B, B), :],
            send_sem=sib_send.at[j], recv_sem=sib_recv.at[j],
            device_id=sibling, device_id_type=MESH,
        )
        c.start()
        sib_out.append(c)
    for st in range(2 * EARLY):
        relay(st, 2)

    scal[8:16, :] = arrived(rz, 3)
    scal[16:24, :] = arrived(tz, 4)
    old = [irow[0:1, :], irow[1:2, :], ocol[...]]
    fr = []
    for k in range(3):
        f = FORGET * old[k] + FRESH * (take(8 + 2 * k) / FF)
        fr.append(f)
        u = take(16 + 2 * k) / f
        snd[5, k : k + 1, :] = u[:, :H] + u[:, H:]
    snd[5, 3:4, :] = scal[22:23, :]
    put(5, 4, fr[0])
    put(5, 6, fr[1])
    exchange(dp2, dp, dp_peers, snd.at[5], 5)
    irow_new[0:1, :] = fr[0]
    irow_new[1:2, :] = fr[1]
    ocol_new[...] = fr[2]
    mean2 = scal[22:23, 3:4] / FF

    for k in range(2):
        rr = lanes_to_rows(lax.rsqrt(fr[k]))
        raw[k] = raw[k] * jnp.concatenate([rr, rr], axis=1)
    raw[2] = raw[2] * lax.rsqrt(fr[2])

    for c in own_tok:
        c.wait()
    for c in sib_out:
        c.wait()
    for st in range(EARLY):
        product(st, y, True)
    for st in range(EARLY):
        products(st, 1)
    for st in range(2 * EARLY):
        relay(st, 3)
    for st in range(EARLY):
        products(st, 2)

    scal[0:8, :] = arrived(dp2, 5)
    s = [jnp.sum(scal[k : k + 1, :], axis=1, keepdims=True) for k in range(3)]
    mean = [jnp.sum(take(4 + 2 * k), axis=1, keepdims=True) / D for k in range(2)] + [mean2]
    coef = []
    for k in range(3):
        clip = jnp.maximum(1.0, jnp.sqrt(s[k] * mean[k] / (D * FF)))
        step = RELATIVE * jnp.sqrt(scal[3:4, k : k + 1] / (D * FF))
        coef.append(step / clip * jnp.sqrt(mean[k]))

    for k in range(2):
        u = raw[k] * (-coef[k])
        upd_v[k] = u
        new_v[k] = w_v[k] + u
    for c in range(EARLY, CHUNKS):
        launch(EARLY + c, new_v, c)

    for st in range(EARLY):
        products(st, 3)
    z_copies = []
    for st in range(EARLY):
        relay(st, 4)
        products(st, 4)
        c = pltpu.make_async_remote_copy(
            src_ref=acc.at[st, pl.ds(B, B), :], dst_ref=zbuf.at[st],
            send_sem=z_send.at[st], recv_sem=z_recv.at[st], device_id=z_pair, device_id_type=MESH,
        )
        c.start()
        z_copies.append(c)

    def z_exchange(st):
        i = st - EARLY
        zout_v[i] = acc[st, B : 2 * B, :].astype(jnp.bfloat16)
        c = pltpu.make_async_remote_copy(
            src_ref=zout_v.at[i], dst_ref=zin_v.at[i],
            send_sem=z_send.at[st], recv_sem=z_recv.at[st], device_id=z_pair, device_id_type=MESH,
        )
        c.start()
        z_copies.append(c)

    u = raw[2] * (-coef[2])
    upd_v[2] = u
    new_v[2] = w_v[2] + u
    outs = [
        pltpu.make_async_copy(new_v.at[pl.ds(0, 2)], inew, out_sem.at[0]),
        pltpu.make_async_copy(upd_v.at[pl.ds(0, 2)], iupd, out_sem.at[1]),
        pltpu.make_async_copy(new_v.at[2], onew, out_sem.at[2]),
        pltpu.make_async_copy(upd_v.at[2], oupd, out_sem.at[3]),
    ]
    for c in outs:
        c.start()

    late = range(2 * EARLY, STREAMS)
    for st in late:
        relay(st, 1)

    rmat[...] = jnp.ones((H, H), jnp.float32)
    for b in range(NY):
        rmat[4 * b : 4 * b + 4, :] = lax.rsqrt(dp2[2 * b + z, 4:8, :])
    rmat[...] = rmat[...].T
    for st in range(EARLY, 2 * EARLY):
        relay(st, 4)
    low = lax.broadcasted_iota(jnp.int32, (H, H), 1) < C64

    def scaled_products(b):
        halves = []
        for h in range(2):
            j = 4 * b + h
            halves.append(
                jnp.where(
                    low,
                    jnp.broadcast_to(rmat[:, j : j + 1], (H, H)),
                    jnp.broadcast_to(rmat[:, j + 2 : j + 3], (H, H)),
                )
            )
        rr = jnp.concatenate(halves, axis=0)
        for st in range(EARLY, 2 * EARLY):
            rows = (agbuf[st, b].astype(jnp.float32) * rr).astype(jnp.bfloat16)
            part = jnp.dot(tokbuf[b], rows, preferred_element_type=jnp.float32)
            if b == 0:
                acc[st] = part
            else:
                acc[st] += part

    for b in range(0, 4):
        scaled_products(b)
    for st in late:
        product(st, y, True)
    for st in late:
        relay(st, 2)
    for b in range(4, NY):
        scaled_products(b)
    for st in range(EARLY, 2 * EARLY):
        z_exchange(st)
    for st in late:
        products(st, 1)
    for st in late:
        relay(st, 3)
    for st in late:
        products(st, 2)
    for st in late:
        products(st, 3)
    for st in late:
        relay(st, 4)
        products(st, 4)
        z_exchange(st)

    lane = lax.broadcasted_iota(jnp.int32, (B, H), 1)
    hid_out = []

    def finish(p, left, right):
        gate = jnp.where(lane < C64, left, pltpu.roll(right, C64, 1))
        up = jnp.where(lane < C64, pltpu.roll(left, C64, 1), right)
        hid_v[p] = (jax.nn.gelu(gate, approximate=True) * up).astype(jnp.bfloat16)
        c = pltpu.make_async_copy(hid_v.at[p], hid.at[:, pl.ds(p * H, H)], out_sem.at[4 + p])
        c.start()
        hid_out.append(c)

    both = []
    for st in range(EARLY):
        lo = st * C64
        z_copies[st].wait_recv()
        z_copies[EARLY + st].wait_recv()
        scale = jnp.concatenate([cc[k][:, lo : lo + C64] * coef[k] for k in range(2)], axis=1)
        step_part = acc[EARLY + st, 0:B, :] + zin_v[st].astype(jnp.float32)
        both.append(acc[st, 0:B, :] + zbuf[st] - step_part * scale)
    finish(0, both[0], both[1])
    both = []
    for st in late:
        z_copies[st].wait_recv()
        both.append(acc[st, 0:B, :] + zin_v[st - EARLY].astype(jnp.float32))
    finish(1, both[0], both[1])

    for stage, slot in enumerate((dp1, rx, tx, rz, tz, dp2)):
        sent(slot, stage)
    for c in tok_out + z_copies:
        c.wait_send()
    for st in range(STREAMS):
        for way in range(2):
            for t in range(1, steps(way, st) + 1):
                ag_copy(way, st, t).wait_send()
    for c in outs + hid_out:
        c.wait()


def copy_kernel(*refs):
    sems = refs[-1]
    n = (len(refs) - 1) // 2
    copies = [pltpu.make_async_copy(refs[i], refs[n + i], sems.at[i]) for i in range(n)]
    for c in copies:
        c.start()
    for c in copies:
        c.wait()


def per_device(tokens, iw, ig, irow, icol, ow, og, orow, ocol):
    f32, bf16 = jnp.float32, jnp.bfloat16
    hbm = pl.BlockSpec(memory_space=pl.ANY)
    vm = pl.BlockSpec(memory_space=pltpu.VMEM)
    sds = jax.ShapeDtypeStruct
    shapes = (
        sds((2, B, B), f32), sds((2, B, B), f32), sds((2, B), f32), sds((2, B), f32),
        sds((B, B), f32), sds((B, B), f32), sds((1, B), f32), sds((1, B), f32), sds((B, B), bf16),
    )
    dma = pltpu.SemaphoreType.DMA
    outs = pl.pallas_call(
        kernel,
        out_shape=shapes,
        in_specs=[hbm, hbm, hbm, vm, vm, hbm, hbm, vm, vm],
        out_specs=(hbm, hbm, vm, vm, hbm, hbm, vm, vm, hbm),
        scratch_shapes=[
            pltpu.VMEM((3, B, B), f32),
            pltpu.VMEM((3, B, B), f32),
            pltpu.VMEM((3, B, B), f32),
            pltpu.VMEM((3, B, B), f32),
            pltpu.VMEM((3, B, B), f32),
            pltpu.VMEM((NY, 2 * B, B), bf16),
            pltpu.VMEM((STREAMS, NY, B, H), bf16),
            pltpu.VMEM((STREAMS, 2 * B, H), f32),
            pltpu.VMEM((EARLY, B, H), f32),
            pltpu.VMEM((CHUNKS, B, H), bf16),
            pltpu.VMEM((CHUNKS, B, H), bf16),
            pltpu.VMEM((CHUNKS // 2, B, H), bf16),
            pltpu.VMEM((16, 8, H), f32),
            pltpu.VMEM((8, 8, H), f32),
            pltpu.VMEM((8, 8, H), f32),
            pltpu.VMEM((8, 8, H), f32),
            pltpu.VMEM((8, 8, H), f32),
            pltpu.VMEM((16, 8, H), f32),
            pltpu.VMEM((6, 8, H), f32),
            pltpu.VMEM((24, H), f32),
            pltpu.VMEM((H, H), f32),
            dma((4,)), dma((NY,)), dma((6,)), dma((6,)), dma((6,)), dma((4,)), dma((4,)), dma((4,)), dma((4,)),
            dma((2, STREAMS, 4)), dma((2, STREAMS, 4)), dma((STREAMS,)), dma((STREAMS,)),
        ],
        compiler_params=pltpu.CompilerParams(
            collective_id=0, has_side_effects=True, vmem_limit_bytes=63 * 1024 * 1024
        ),
        cost_estimate=pl.CostEstimate(
            flops=2 * B * D * 2 * B, bytes_accessed=5 * 1024 * 1024, transcendentals=B * B
        ),
    )(tokens, iw, ig, irow, icol, ow, og, orow.reshape(1, B), ocol.reshape(1, B))
    outs = pl.pallas_call(
        copy_kernel,
        out_shape=shapes,
        in_specs=[hbm] * len(shapes),
        out_specs=(hbm,) * len(shapes),
        scratch_shapes=[dma((len(shapes),))],
    )(*outs)
    outs = list(outs)
    outs[6] = outs[6].reshape(B)
    outs[7] = outs[7].reshape(B)
    return tuple(outs)


def solution(mesh):
    placed = (
        P("dp", None),
        P(None, "dp", "mp"),
        P(None, "dp", "mp"),
        P(None, "dp"),
        P(None, "mp"),
        P("mp", "dp"),
        P("mp", "dp"),
        P("mp"),
        P("dp"),
    )
    return jax.shard_map(
        per_device,
        mesh=mesh,
        in_specs=placed,
        out_specs=(
            P(None, "dp", "mp"),
            P(None, "dp", "mp"),
            P(None, "dp"),
            P(None, "mp"),
            P("mp", "dp"),
            P("mp", "dp"),
            P("mp"),
            P("dp"),
            P("dp", "mp"),
        ),
        check_vma=False,
    )
```

```python
import functools

import jax
import jax.numpy as jnp
from jax import lax
from jax.experimental import pallas as pl
from jax.experimental.pallas import tpu as pltpu
from jax.sharding import PartitionSpec as P

D = 4096
FF = 16384
STEP = 10
FORGET = 1.0 - STEP ** (-0.8)
FRESH = 1.0 - FORGET
RELATIVE = min(0.01, STEP ** (-0.5))

NY = 8
B = 256
H = 128
CHUNKS = 4
EARLY = 2
STREAMS = 2 * EARLY + CHUNKS - EARLY
C64 = 64
MESH = pl.DeviceIdType.MESH


def rows_to_lanes(q):
    return jnp.sum((q[:, :H] + q[:, H:]).T, axis=0, keepdims=True)


def lanes_to_rows(v):
    return jnp.concatenate(
        [jnp.broadcast_to(v[:, :H], (H, H)).T, jnp.broadcast_to(v[:, H:], (H, H)).T], axis=0
    )


def far_first(n):
    return sorted(range(1, n), key=lambda k: -min(k, n - k))


def kernel(
    tok, iw, ig, irow, icol, ow, og, orow, ocol,
    inew, iupd, irow_new, icol_new, onew, oupd, orow_new, ocol_new, hid,
    g_v, w_v, raw, tokbuf, agbuf, acc, zbuf, zout_v, zin_v,
    dp1, rx, rz, tx, tz, dp2, snd, scal, rmat,
    load_sem, tok_sem, st_send, st_recv, tx_send, tx_recv, sib_send, sib_recv,
    ag_send, ag_recv, z_send, z_recv,
):
    dp, mp = lax.axis_index("dp"), lax.axis_index("mp")
    y, z = dp // 2, lax.rem(dp, 2)
    x, zc = mp // 8, lax.rem(mp, 8)
    core = lax.rem(mp, 2)

    dp_peers = [(lax.rem(dp + k, 16), mp) for k in far_first(16)]
    x_peers = [(dp, lax.rem(x + k, 8) * 8 + zc) for k in far_first(8)]
    zc_peers = [(dp, x * 8 + lax.rem(zc + k, 8)) for k in far_first(8)]
    y_next = (lax.rem(y + 1, NY) * 2 + z, mp)
    y_prev = (lax.rem(y + NY - 1, NY) * 2 + z, mp)
    z_pair = (y * 2 + 1 - z, mp)
    sibling = (dp, mp + 1 - 2 * core)

    loads = [
        pltpu.make_async_copy(ig, g_v.at[pl.ds(0, 2)], load_sem.at[0]),
        pltpu.make_async_copy(og, g_v.at[2], load_sem.at[1]),
        pltpu.make_async_copy(iw, w_v.at[pl.ds(0, 2)], load_sem.at[2]),
        pltpu.make_async_copy(ow, w_v.at[2], load_sem.at[3]),
    ]
    for c in loads:
        c.start()

    barrier = pltpu.get_barrier_semaphore()
    for peer in dp_peers + x_peers + zc_peers:
        pl.semaphore_signal(barrier, inc=1, device_id=peer, device_id_type=MESH)

    def put(i, row, v):
        snd[i, row : row + 1, :] = v[:, :H]
        snd[i, row + 1 : row + 2, :] = v[:, H:]

    def take(row):
        return jnp.concatenate([scal[row : row + 1, :], scal[row + 1 : row + 2, :]], axis=1)

    def exchange(slot, me, peers, src, stage):
        for p in peers:
            pltpu.make_async_remote_copy(
                src_ref=src, dst_ref=slot.at[me], send_sem=st_send.at[stage], recv_sem=st_recv.at[stage],
                device_id=p, device_id_type=MESH,
            ).start()
        slot[me] = src[...]

    def arrived(slot, stage):
        n = slot.shape[0]
        part = slot.at[pl.ds(0, n - 1)]
        pltpu.make_async_copy(part, part, st_recv.at[stage]).wait()
        tot = slot[0]
        for i in range(1, n):
            tot = tot + slot[i]
        return tot

    def sent(slot, stage):
        part = slot.at[pl.ds(0, slot.shape[0] - 1)]
        pltpu.make_async_copy(part, part, st_send.at[stage]).wait()

    def ag_copy(way, st, s):
        src = lax.rem(y + NY - (s - 1), NY) if way == 0 else lax.rem(y + s - 1, NY)
        return pltpu.make_async_remote_copy(
            src_ref=agbuf.at[st, src], dst_ref=agbuf.at[st, src],
            send_sem=ag_send.at[way, st, s - 1], recv_sem=ag_recv.at[way, st, s - 1],
            device_id=y_next if way == 0 else y_prev, device_id_type=MESH,
        )

    def steps(way, st):
        return 4 if (st % 2 == 0) == (way == 0) else 3

    def origin(way, s):
        return lax.rem(y + NY - s, NY) if way == 0 else lax.rem(y + s, NY)

    def launch(st, pair, c):
        lo = c * C64
        block = jnp.concatenate([pair[0, :, lo : lo + C64], pair[1, :, lo : lo + C64]], axis=1)
        agbuf[st, y] = block.astype(jnp.bfloat16)
        for way in range(2):
            ag_copy(way, st, 1).start()

    def relay(st, s):
        for way in range(2):
            if s <= steps(way, st):
                ag_copy(way, st, s).wait_recv()
                if s < steps(way, st):
                    ag_copy(way, st, s + 1).start()

    def product(st, b, first=False):
        part = jnp.dot(tokbuf[b], agbuf[st, b], preferred_element_type=jnp.float32)
        if first:
            acc[st] = part
        else:
            acc[st] += part

    def products(st, s):
        for way in range(2):
            if s <= steps(way, st):
                product(st, origin(way, s))

    snd[...] = jnp.zeros_like(snd)
    loads[0].wait()
    for k in range(2):
        g = g_v[k]
        put(0, 2 * k, jnp.sum(g * g + 1e-30, axis=0, keepdims=True))
    loads[1].wait()
    g = g_v[2]
    put(0, 4, rows_to_lanes(g * g + 1e-30))

    pl.semaphore_wait(barrier, 29)
    exchange(dp1, dp, dp_peers, snd.at[0], 0)

    loads[2].wait()
    for c in range(EARLY):
        launch(c, w_v, c)
    launch(EARLY, g_v, 0)
    own_tok = []
    for b in range(NY):
        c = pltpu.make_async_copy(
            tok.at[:, pl.ds(pl.multiple_of((2 * b + z) * B, B), B)],
            tokbuf.at[b, pl.ds(0, B), :],
            tok_sem.at[b],
        )
        c.start()
        own_tok.append(c)

    tok_out = []
    for j in range(4):
        b = core * 4 + j
        c = pltpu.make_async_remote_copy(
            src_ref=tok.at[:, pl.ds(pl.multiple_of((2 * b + 1 - z) * B, B), B)],
            dst_ref=tokbuf.at[b, pl.ds(B, B), :],
            send_sem=tx_send.at[j], recv_sem=tx_recv.at[j],
            device_id=z_pair, device_id_type=MESH,
        )
        c.start()
        tok_out.append(c)

    for k in range(2):
        g = g_v[k]
        put(1, 2 * k, rows_to_lanes(g * g + 1e-30))
    g = g_v[2]
    put(1, 4, jnp.sum(g * g + 1e-30, axis=0, keepdims=True))
    exchange(rx, x, x_peers, snd.at[1], 1)
    loads[3].wait()
    lane1 = lax.broadcasted_iota(jnp.int32, (1, H), 1)
    misc = jnp.zeros((1, H), jnp.float32)
    for k in range(3):
        w = w_v[k]
        v = jnp.sum(w * w, axis=0, keepdims=True)
        misc = jnp.where(lane1 == k, jnp.sum(v, axis=1, keepdims=True), misc)

    scal[0:8, :] = arrived(dp1, 0)
    relay(0, 1)
    old = [icol[0:1, :], icol[1:2, :], orow[...]]
    fc = [FORGET * old[k] + FRESH * (take(2 * k) / D) for k in range(3)]
    cc = [lax.rsqrt(f) for f in fc]
    misc = jnp.where(lane1 == 3, jnp.sum(fc[2], axis=1, keepdims=True), misc)
    snd[2, 6:7, :] = misc
    for k in range(2):
        g = g_v[k] * cc[k]
        raw[k] = g
        put(2, 2 * k, rows_to_lanes(g * g))
    c2 = lanes_to_rows(cc[2])
    g = g_v[2] * jnp.concatenate([c2, c2], axis=1)
    raw[2] = g
    put(2, 4, jnp.sum(g * g, axis=0, keepdims=True))
    exchange(tx, x, x_peers, snd.at[2], 2)
    icol_new[0:1, :] = fc[0]
    icol_new[1:2, :] = fc[1]
    orow_new[...] = fc[2]

    relay(1, 1)
    launch(EARLY + 1, g_v, 1)
    snd[3] = arrived(rx, 1)
    exchange(rz, zc, zc_peers, snd.at[3], 3)
    relay(2, 1)
    relay(0, 2)
    relay(1, 2)
    snd[4] = arrived(tx, 2)
    exchange(tz, zc, zc_peers, snd.at[4], 4)
    relay(3, 1)
    relay(0, 3)
    relay(1, 3)

    scal[8:16, :] = arrived(rz, 3)
    scal[16:24, :] = arrived(tz, 4)
    old = [irow[0:1, :], irow[1:2, :], ocol[...]]
    fr = []
    for k in range(3):
        f = FORGET * old[k] + FRESH * (take(8 + 2 * k) / FF)
        fr.append(f)
        u = take(16 + 2 * k) / f
        snd[5, k : k + 1, :] = u[:, :H] + u[:, H:]
    snd[5, 3:4, :] = scal[22:23, :]
    put(5, 4, fr[0])
    put(5, 6, fr[1])
    exchange(dp2, dp, dp_peers, snd.at[5], 5)
    irow_new[0:1, :] = fr[0]
    irow_new[1:2, :] = fr[1]
    ocol_new[...] = fr[2]
    mean2 = scal[22:23, 3:4] / FF

    for k in range(2):
        rr = lanes_to_rows(lax.rsqrt(fr[k]))
        raw[k] = raw[k] * jnp.concatenate([rr, rr], axis=1)
    raw[2] = raw[2] * lax.rsqrt(fr[2])

    relay(2, 2)

    sib_out = []
    for j in range(4):
        b = core * 4 + j
        tok_out[j].wait_recv()
        c = pltpu.make_async_remote_copy(
            src_ref=tokbuf.at[b, pl.ds(B, B), :],
            dst_ref=tokbuf.at[b, pl.ds(B, B), :],
            send_sem=sib_send.at[j], recv_sem=sib_recv.at[j],
            device_id=sibling, device_id_type=MESH,
        )
        c.start()
        sib_out.append(c)
    relay(3, 2)

    for c in own_tok:
        c.wait()
    for c in sib_out:
        c.wait()
    for st in range(EARLY):
        product(st, y, True)
        for t in range(1, 4):
            products(st, t)
    relay(2, 3)

    scal[0:8, :] = arrived(dp2, 5)
    s = [jnp.sum(scal[k : k + 1, :], axis=1, keepdims=True) for k in range(3)]
    mean = [jnp.sum(take(4 + 2 * k), axis=1, keepdims=True) / D for k in range(2)] + [mean2]
    coef = []
    for k in range(3):
        clip = jnp.maximum(1.0, jnp.sqrt(s[k] * mean[k] / (D * FF)))
        step = RELATIVE * jnp.sqrt(scal[3:4, k : k + 1] / (D * FF))
        coef.append(step / clip * jnp.sqrt(mean[k]))

    late = range(2 * EARLY, STREAMS)
    for cols in (pl.ds(EARLY * C64, B - EARLY * C64), pl.ds(0, EARLY * C64)):
        for k in range(2):
            u = raw[k, :, cols] * (-coef[k])
            iupd[k, :, cols] = u
            inew[k, :, cols] = w_v[k, :, cols] + u
        if cols.start:
            for st in late:
                launch(st, inew, st - EARLY)

    def z_exchange(st):
        i = st - EARLY
        zout_v[i] = acc[st, B : 2 * B, :].astype(jnp.bfloat16)
        c = pltpu.make_async_remote_copy(
            src_ref=zout_v.at[i], dst_ref=zin_v.at[i],
            send_sem=z_send.at[st], recv_sem=z_recv.at[st], device_id=z_pair, device_id_type=MESH,
        )
        c.start()
        z_copies.append(c)

    relay(3, 3)
    z_copies = []
    for st in range(EARLY):
        relay(st, 4)
        products(st, 4)
        c = pltpu.make_async_remote_copy(
            src_ref=acc.at[st, pl.ds(B, B), :], dst_ref=zbuf.at[st],
            send_sem=z_send.at[st], recv_sem=z_recv.at[st], device_id=z_pair, device_id_type=MESH,
        )
        c.start()
        z_copies.append(c)
    u = raw[2] * (-coef[2])
    oupd[...] = u
    onew[...] = w_v[2] + u

    rmat[...] = jnp.ones((H, H), jnp.float32)
    for b in range(NY):
        rmat[4 * b : 4 * b + 4, :] = lax.rsqrt(dp2[2 * b + z, 4:8, :])
    rmat[...] = rmat[...].T
    for st in range(EARLY, 2 * EARLY):
        relay(st, 4)
    low = lax.broadcasted_iota(jnp.int32, (H, H), 1) < C64

    def scaled_products(b):
        halves = []
        for h in range(2):
            j = 4 * b + h
            halves.append(
                jnp.where(
                    low,
                    jnp.broadcast_to(rmat[:, j : j + 1], (H, H)),
                    jnp.broadcast_to(rmat[:, j + 2 : j + 3], (H, H)),
                )
            )
        rr = jnp.concatenate(halves, axis=0)
        for st in range(EARLY, 2 * EARLY):
            rows = (agbuf[st, b].astype(jnp.float32) * rr).astype(jnp.bfloat16)
            part = jnp.dot(tokbuf[b], rows, preferred_element_type=jnp.float32)
            if b == 0:
                acc[st] = part
            else:
                acc[st] += part

    for b in range(0, 3):
        scaled_products(b)
    for st in late:
        relay(st, 1)
    for b in range(3, 6):
        scaled_products(b)
    for st in late:
        relay(st, 2)
    for b in range(6, NY):
        scaled_products(b)
    for st in range(EARLY, 2 * EARLY):
        z_exchange(st)
    for st in late:
        product(st, y, True)
        products(st, 1)
    for st in late:
        relay(st, 3)
    for st in late:
        products(st, 2)
        products(st, 3)
    for st in late:
        relay(st, 4)
        products(st, 4)
        z_exchange(st)

    lane = lax.broadcasted_iota(jnp.int32, (B, H), 1)

    def finish(p, left, right):
        gate = jnp.where(lane < C64, left, pltpu.roll(right, C64, 1))
        up = jnp.where(lane < C64, pltpu.roll(left, C64, 1), right)
        hid[:, p * H : (p + 1) * H] = (jax.nn.gelu(gate, approximate=True) * up).astype(jnp.bfloat16)

    both = []
    for st in range(EARLY):
        lo = st * C64
        z_copies[st].wait_recv()
        z_copies[EARLY + st].wait_recv()
        scale = jnp.concatenate([cc[k][:, lo : lo + C64] * coef[k] for k in range(2)], axis=1)
        step_part = acc[EARLY + st, 0:B, :] + zin_v[st].astype(jnp.float32)
        both.append(acc[st, 0:B, :] + zbuf[st] - step_part * scale)
    finish(0, both[0], both[1])
    both = []
    for st in late:
        z_copies[st].wait_recv()
        both.append(acc[st, 0:B, :] + zin_v[st - EARLY].astype(jnp.float32))
    finish(1, both[0], both[1])

    for stage, slot in enumerate((dp1, rx, tx, rz, tz, dp2)):
        sent(slot, stage)
    for c in tok_out + z_copies:
        c.wait_send()
    for st in range(STREAMS):
        for way in range(2):
            for t in range(1, steps(way, st) + 1):
                ag_copy(way, st, t).wait_send()


def copy_kernel(*refs):
    sems = refs[-1]
    n = (len(refs) - 1) // 2
    copies = [pltpu.make_async_copy(refs[i], refs[n + i], sems.at[i]) for i in range(n)]
    for c in copies:
        c.start()
    for c in copies:
        c.wait()


def per_device(tokens, iw, ig, irow, icol, ow, og, orow, ocol):
    f32, bf16 = jnp.float32, jnp.bfloat16
    hbm = pl.BlockSpec(memory_space=pl.ANY)
    vm = pl.BlockSpec(memory_space=pltpu.VMEM)
    sds = jax.ShapeDtypeStruct
    shapes = (
        sds((2, B, B), f32), sds((2, B, B), f32), sds((2, B), f32), sds((2, B), f32),
        sds((B, B), f32), sds((B, B), f32), sds((1, B), f32), sds((1, B), f32), sds((B, B), bf16),
    )
    dma = pltpu.SemaphoreType.DMA
    outs = pl.pallas_call(
        kernel,
        out_shape=tuple(pltpu.VMEM(a.shape, a.dtype) for a in shapes),
        in_specs=[hbm, hbm, hbm, vm, vm, hbm, hbm, vm, vm],
        out_specs=(vm,) * len(shapes),
        scratch_shapes=[
            pltpu.VMEM((3, B, B), f32),
            pltpu.VMEM((3, B, B), f32),
            pltpu.VMEM((3, B, B), f32),
            pltpu.VMEM((NY, 2 * B, B), bf16),
            pltpu.VMEM((STREAMS, NY, B, H), bf16),
            pltpu.VMEM((STREAMS, 2 * B, H), f32),
            pltpu.VMEM((EARLY, B, H), f32),
            pltpu.VMEM((CHUNKS, B, H), bf16),
            pltpu.VMEM((CHUNKS, B, H), bf16),
            pltpu.VMEM((16, 8, H), f32),
            pltpu.VMEM((8, 8, H), f32),
            pltpu.VMEM((8, 8, H), f32),
            pltpu.VMEM((8, 8, H), f32),
            pltpu.VMEM((8, 8, H), f32),
            pltpu.VMEM((16, 8, H), f32),
            pltpu.VMEM((6, 8, H), f32),
            pltpu.VMEM((24, H), f32),
            pltpu.VMEM((H, H), f32),
            dma((4,)), dma((NY,)), dma((6,)), dma((6,)), dma((4,)), dma((4,)), dma((4,)), dma((4,)),
            dma((2, STREAMS, 4)), dma((2, STREAMS, 4)), dma((STREAMS,)), dma((STREAMS,)),
        ],
        compiler_params=pltpu.CompilerParams(
            collective_id=0, has_side_effects=True, vmem_limit_bytes=61 * 1024 * 1024
        ),
        cost_estimate=pl.CostEstimate(
            flops=2 * B * D * 2 * B, bytes_accessed=5 * 1024 * 1024, transcendentals=B * B
        ),
    )(tokens, iw, ig, irow, icol, ow, og, orow.reshape(1, B), ocol.reshape(1, B))
    outs = pl.pallas_call(
        copy_kernel,
        out_shape=shapes,
        in_specs=[vm] * len(shapes),
        out_specs=(hbm,) * len(shapes),
        scratch_shapes=[dma((len(shapes),))],
    )(*[pltpu.with_memory_space_constraint(o, pltpu.VMEM) for o in outs])
    outs = list(outs)
    outs[6] = outs[6].reshape(B)
    outs[7] = outs[7].reshape(B)
    return tuple(outs)


def solution(mesh):
    placed = (
        P("dp", None),
        P(None, "dp", "mp"),
        P(None, "dp", "mp"),
        P(None, "dp"),
        P(None, "mp"),
        P("mp", "dp"),
        P("mp", "dp"),
        P("mp"),
        P("dp"),
    )
    return jax.shard_map(
        per_device,
        mesh=mesh,
        in_specs=placed,
        out_specs=(
            P(None, "dp", "mp"),
            P(None, "dp", "mp"),
            P(None, "dp"),
            P(None, "mp"),
            P("mp", "dp"),
            P("mp", "dp"),
            P("mp"),
            P("dp"),
            P("dp", "mp"),
        ),
        check_vma=False,
    )
```

```python
import functools

import jax
import jax.numpy as jnp
from jax import lax
from jax.experimental import pallas as pl
from jax.experimental.pallas import tpu as pltpu
from jax.sharding import PartitionSpec as P

D = 4096
FF = 16384
STEP = 10
FORGET = 1.0 - STEP ** (-0.8)
FRESH = 1.0 - FORGET
RELATIVE = min(0.01, STEP ** (-0.5))

NY = 8
B = 256
H = 128
CHUNKS = 4
EARLY = 2
STREAMS = 2 * EARLY + CHUNKS - EARLY
C64 = 64
MESH = pl.DeviceIdType.MESH


def rows_to_lanes(q):
    return jnp.sum((q[:, :H] + q[:, H:]).T, axis=0, keepdims=True)


def lanes_to_rows(v):
    return jnp.concatenate(
        [jnp.broadcast_to(v[:, :H], (H, H)).T, jnp.broadcast_to(v[:, H:], (H, H)).T], axis=0
    )


def far_first(n):
    return sorted(range(1, n), key=lambda k: -min(k, n - k))


def kernel(
    tok, iw, ig, irow, icol, ow, og, orow, ocol,
    inew, iupd, irow_new, icol_new, onew, oupd, orow_new, ocol_new, hid,
    g_v, w_v, raw, late_w, late_raw, tokbuf, tok_far, xbuf, agbuf, acc, zbuf, zout_v, zin_v,
    dp1, rx, rz, tx, tz, dp2, snd, scal, rmat,
    load_sem, tok_sem, st_send, st_recv, tx_send, tx_recv, sib_send, sib_recv,
    ag_send, ag_recv, x_send, x_recv, z_send, z_recv,
):
    dp, mp = lax.axis_index("dp"), lax.axis_index("mp")
    y, z = dp // 2, lax.rem(dp, 2)
    x, zc = mp // 8, lax.rem(mp, 8)
    core = lax.rem(mp, 2)

    dp_peers = [(lax.rem(dp + k, 16), mp) for k in far_first(16)]
    x_peers = [(dp, lax.rem(x + k, 8) * 8 + zc) for k in far_first(8)]
    zc_peers = [(dp, x * 8 + lax.rem(zc + k, 8)) for k in far_first(8)]
    y_next = (lax.rem(y + 1, NY) * 2 + z, mp)
    y_prev = (lax.rem(y + NY - 1, NY) * 2 + z, mp)
    z_pair = (y * 2 + 1 - z, mp)
    y_next_pair = (lax.rem(y + 1, NY) * 2 + 1 - z, mp)
    y_prev_pair = (lax.rem(y + NY - 1, NY) * 2 + 1 - z, mp)
    across = lax.rem(y + 4, NY)
    sibling = (dp, mp + 1 - 2 * core)

    loads = [
        pltpu.make_async_copy(ig, g_v.at[pl.ds(0, 2)], load_sem.at[0]),
        pltpu.make_async_copy(og, g_v.at[2], load_sem.at[1]),
        pltpu.make_async_copy(iw, w_v.at[pl.ds(0, 2)], load_sem.at[2]),
        pltpu.make_async_copy(ow, w_v.at[2], load_sem.at[3]),
    ]
    for c in loads:
        c.start()

    barrier = pltpu.get_barrier_semaphore()
    for peer in dp_peers + x_peers + zc_peers:
        pl.semaphore_signal(barrier, inc=1, device_id=peer, device_id_type=MESH)

    def put(i, row, v):
        snd[i, row : row + 1, :] = v[:, :H]
        snd[i, row + 1 : row + 2, :] = v[:, H:]

    def take(row):
        return jnp.concatenate([scal[row : row + 1, :], scal[row + 1 : row + 2, :]], axis=1)

    def exchange(slot, me, peers, src, stage):
        for p in peers:
            pltpu.make_async_remote_copy(
                src_ref=src, dst_ref=slot.at[me], send_sem=st_send.at[stage], recv_sem=st_recv.at[stage],
                device_id=p, device_id_type=MESH,
            ).start()
        slot[me] = src[...]

    def arrived(slot, stage):
        n = slot.shape[0]
        part = slot.at[pl.ds(0, n - 1)]
        pltpu.make_async_copy(part, part, st_recv.at[stage]).wait()
        tot = slot[0]
        for i in range(1, n):
            tot = tot + slot[i]
        return tot

    def sent(slot, stage):
        part = slot.at[pl.ds(0, slot.shape[0] - 1)]
        pltpu.make_async_copy(part, part, st_send.at[stage]).wait()

    def ag_copy(way, st, s, h):
        src = lax.rem(y + NY - (s - 1), NY) if way == 0 else lax.rem(y + s - 1, NY)
        rows = B // pieces(st)
        part = agbuf.at[st, src, pl.ds(h * rows, rows), :]
        return pltpu.make_async_remote_copy(
            src_ref=part, dst_ref=part,
            send_sem=ag_send.at[way, st, s - 1, h], recv_sem=ag_recv.at[way, st, s - 1, h],
            device_id=y_next if way == 0 else y_prev, device_id_type=MESH,
        )

    def pieces(st):
        return 1 if st < 2 * EARLY else 2

    def steps(way, st):
        return 4 if (st % 2 == 0) == (way == 0) else 3

    def origin(way, s):
        return lax.rem(y + NY - s, NY) if way == 0 else lax.rem(y + s, NY)

    def pack(pair, c):
        lo = c * C64
        return jnp.concatenate([pair[0, :, lo : lo + C64], pair[1, :, lo : lo + C64]], axis=1)

    def launch(st, block):
        agbuf[st, y] = block.astype(jnp.bfloat16)
        for h in range(pieces(st)):
            for way in range(2):
                ag_copy(way, st, 1, h).start()

    def far_copy(way, st, h):
        rows = B // pieces(st)
        src = lax.rem(y + NY - 3, NY) if way == 0 else lax.rem(y + 3, NY)
        return pltpu.make_async_remote_copy(
            src_ref=agbuf.at[st, src, pl.ds(h * rows, rows), :],
            dst_ref=xbuf.at[st - 2 * EARLY, pl.ds(h * rows, rows), :],
            send_sem=x_send.at[st - 2 * EARLY, h], recv_sem=x_recv.at[st - 2 * EARLY, h],
            device_id=y_next_pair if way == 0 else y_prev_pair, device_id_type=MESH,
        )

    def far_way(st):
        return 0 if steps(0, st) == 4 else 1

    def relay(st, s):
        for h in range(pieces(st)):
            for way in range(2):
                if s <= steps(way, st):
                    ag_copy(way, st, s, h).wait_recv()
                    if s < steps(way, st):
                        ag_copy(way, st, s + 1, h).start()
                        if s == 3 and st >= 2 * EARLY:
                            far_copy(way, st, h).start()

    def product(st, b, first=False):
        part = jnp.dot(tokbuf[b], agbuf[st, b], preferred_element_type=jnp.float32)
        if first:
            acc[st] = part
        else:
            acc[st] += part

    def products(st, s):
        for way in range(2):
            if s <= steps(way, st):
                product(st, origin(way, s))

    snd[...] = jnp.zeros_like(snd)
    loads[0].wait()
    for k in range(2):
        g = g_v[k]
        put(0, 2 * k, jnp.sum(g * g + 1e-30, axis=0, keepdims=True))
    loads[1].wait()
    g = g_v[2]
    put(0, 4, rows_to_lanes(g * g + 1e-30))

    pl.semaphore_wait(barrier, 29)
    exchange(dp1, dp, dp_peers, snd.at[0], 0)

    loads[2].wait()
    for c in range(EARLY):
        launch(c, pack(w_v, c))
    for c in range(EARLY):
        launch(EARLY + c, pack(g_v, c))
    own_tok = [
        pltpu.make_async_copy(
            tok.at[:, pl.ds(pl.multiple_of((2 * across + 1 - z) * B, B), B)], tok_far, tok_sem.at[NY]
        )
    ]
    own_tok[0].start()
    for b in range(NY):
        c = pltpu.make_async_copy(
            tok.at[:, pl.ds(pl.multiple_of((2 * b + z) * B, B), B)],
            tokbuf.at[b, pl.ds(0, B), :],
            tok_sem.at[b],
        )
        c.start()
        own_tok.append(c)

    tok_out = []
    for j in range(4):
        b = core * 4 + j
        c = pltpu.make_async_remote_copy(
            src_ref=tok.at[:, pl.ds(pl.multiple_of((2 * b + 1 - z) * B, B), B)],
            dst_ref=tokbuf.at[b, pl.ds(B, B), :],
            send_sem=tx_send.at[j], recv_sem=tx_recv.at[j],
            device_id=z_pair, device_id_type=MESH,
        )
        c.start()
        tok_out.append(c)

    for k in range(2):
        g = g_v[k]
        put(1, 2 * k, rows_to_lanes(g * g + 1e-30))
    g = g_v[2]
    put(1, 4, jnp.sum(g * g + 1e-30, axis=0, keepdims=True))
    exchange(rx, x, x_peers, snd.at[1], 1)
    loads[3].wait()
    lane1 = lax.broadcasted_iota(jnp.int32, (1, H), 1)
    misc = jnp.zeros((1, H), jnp.float32)
    for k in range(3):
        w = w_v[k]
        v = jnp.sum(w * w, axis=0, keepdims=True)
        misc = jnp.where(lane1 == k, jnp.sum(v, axis=1, keepdims=True), misc)

    scal[0:8, :] = arrived(dp1, 0)
    relay(0, 1)
    old = [icol[0:1, :], icol[1:2, :], orow[...]]
    fc = [FORGET * old[k] + FRESH * (take(2 * k) / D) for k in range(3)]
    cc = [lax.rsqrt(f) for f in fc]
    misc = jnp.where(lane1 == 3, jnp.sum(fc[2], axis=1, keepdims=True), misc)
    snd[2, 6:7, :] = misc
    for k in range(2):
        g = g_v[k] * cc[k]
        raw[k] = g
        put(2, 2 * k, rows_to_lanes(g * g))
    c2 = lanes_to_rows(cc[2])
    g = g_v[2] * jnp.concatenate([c2, c2], axis=1)
    raw[2] = g
    put(2, 4, jnp.sum(g * g, axis=0, keepdims=True))
    exchange(tx, x, x_peers, snd.at[2], 2)
    icol_new[0:1, :] = fc[0]
    icol_new[1:2, :] = fc[1]
    orow_new[...] = fc[2]

    relay(1, 1)
    snd[3] = arrived(rx, 1)
    exchange(rz, zc, zc_peers, snd.at[3], 3)
    relay(2, 1)
    relay(3, 1)
    relay(0, 2)
    snd[4] = arrived(tx, 2)
    exchange(tz, zc, zc_peers, snd.at[4], 4)
    relay(1, 2)
    relay(2, 2)
    relay(3, 2)
    relay(0, 3)

    scal[8:16, :] = arrived(rz, 3)
    scal[16:24, :] = arrived(tz, 4)
    old = [irow[0:1, :], irow[1:2, :], ocol[...]]
    fr = []
    for k in range(3):
        f = FORGET * old[k] + FRESH * (take(8 + 2 * k) / FF)
        fr.append(f)
        u = take(16 + 2 * k) / f
        snd[5, k : k + 1, :] = u[:, :H] + u[:, H:]
    snd[5, 3:4, :] = scal[22:23, :]
    put(5, 4, fr[0])
    put(5, 6, fr[1])
    exchange(dp2, dp, dp_peers, snd.at[5], 5)
    irow_new[0:1, :] = fr[0]
    irow_new[1:2, :] = fr[1]
    ocol_new[...] = fr[2]
    mean2 = scal[22:23, 3:4] / FF

    for k in range(2):
        rr = lanes_to_rows(lax.rsqrt(fr[k]))
        raw[k] = raw[k] * jnp.concatenate([rr, rr], axis=1)
    raw[2] = raw[2] * lax.rsqrt(fr[2])
    relay(1, 3)

    sib_out = []
    for j in range(4):
        b = core * 4 + j
        tok_out[j].wait_recv()
        c = pltpu.make_async_remote_copy(
            src_ref=tokbuf.at[b, pl.ds(B, B), :],
            dst_ref=tokbuf.at[b, pl.ds(B, B), :],
            send_sem=sib_send.at[j], recv_sem=sib_recv.at[j],
            device_id=sibling, device_id_type=MESH,
        )
        c.start()
        sib_out.append(c)
    relay(2, 3)
    late = range(2 * EARLY, STREAMS)
    for st in late:
        late_w[st - 2 * EARLY] = pack(w_v, st - EARLY)
        late_raw[st - 2 * EARLY] = pack(raw, st - EARLY)
    relay(3, 3)

    for c in own_tok:
        c.wait()
    for c in sib_out:
        c.wait()
    for st in range(EARLY):
        product(st, y, True)
        for t in range(1, 4):
            products(st, t)

    scal[0:8, :] = arrived(dp2, 5)
    s = [jnp.sum(scal[k : k + 1, :], axis=1, keepdims=True) for k in range(3)]
    mean = [jnp.sum(take(4 + 2 * k), axis=1, keepdims=True) / D for k in range(2)] + [mean2]
    coef = []
    for k in range(3):
        clip = jnp.maximum(1.0, jnp.sqrt(s[k] * mean[k] / (D * FF)))
        step = RELATIVE * jnp.sqrt(scal[3:4, k : k + 1] / (D * FF))
        coef.append(step / clip * jnp.sqrt(mean[k]))

    both_coef = jnp.where(lane1 < C64, coef[0], coef[1])
    for st in late:
        i = st - 2 * EARLY
        launch(st, late_w[i] + late_raw[i] * (-both_coef))
    for k in range(2):
        u = raw[k] * (-coef[k])
        iupd[k] = u
        inew[k] = w_v[k] + u

    def z_exchange(st):
        i = st - EARLY
        zout_v[i] = acc[st, B : 2 * B, :].astype(jnp.bfloat16)
        c = pltpu.make_async_remote_copy(
            src_ref=zout_v.at[i], dst_ref=zin_v.at[i],
            send_sem=z_send.at[st], recv_sem=z_recv.at[st], device_id=z_pair, device_id_type=MESH,
        )
        c.start()
        z_copies.append(c)

    z_copies = []
    for st in range(EARLY):
        relay(st, 4)
        products(st, 4)
        c = pltpu.make_async_remote_copy(
            src_ref=acc.at[st, pl.ds(B, B), :], dst_ref=zbuf.at[st],
            send_sem=z_send.at[st], recv_sem=z_recv.at[st], device_id=z_pair, device_id_type=MESH,
        )
        c.start()
        z_copies.append(c)
    u = raw[2] * (-coef[2])
    oupd[...] = u
    onew[...] = w_v[2] + u

    rmat[...] = jnp.ones((H, H), jnp.float32)
    for b in range(NY):
        rmat[4 * b : 4 * b + 4, :] = lax.rsqrt(dp2[2 * b + z, 4:8, :])
    rmat[...] = rmat[...].T
    for st in range(EARLY, 2 * EARLY):
        relay(st, 4)
    low = lax.broadcasted_iota(jnp.int32, (H, H), 1) < C64

    def scaled_products(b):
        halves = []
        for h in range(2):
            j = 4 * b + h
            halves.append(
                jnp.where(
                    low,
                    jnp.broadcast_to(rmat[:, j : j + 1], (H, H)),
                    jnp.broadcast_to(rmat[:, j + 2 : j + 3], (H, H)),
                )
            )
        rr = jnp.concatenate(halves, axis=0)
        for st in range(EARLY, 2 * EARLY):
            rows = (agbuf[st, b].astype(jnp.float32) * rr).astype(jnp.bfloat16)
            part = jnp.dot(tokbuf[b], rows, preferred_element_type=jnp.float32)
            if b == 0:
                acc[st] = part
            else:
                acc[st] += part

    for b in range(0, 3):
        scaled_products(b)
    for st in late:
        relay(st, 1)
    for b in range(3, 6):
        scaled_products(b)
    for st in late:
        relay(st, 2)
    for b in range(6, NY):
        scaled_products(b)
    for st in range(EARLY, 2 * EARLY):
        z_exchange(st)
    for st in late:
        product(st, y, True)
        products(st, 1)
        products(st, 2)
    for st in late:
        relay(st, 3)
    for st in late:
        products(st, 3)
        z_exchange(st)

    lane = lax.broadcasted_iota(jnp.int32, (B, H), 1)

    def finish(p, left, right):
        gate = jnp.where(lane < C64, left, pltpu.roll(right, C64, 1))
        up = jnp.where(lane < C64, pltpu.roll(left, C64, 1), right)
        hid[:, p * H : (p + 1) * H] = (jax.nn.gelu(gate, approximate=True) * up).astype(jnp.bfloat16)

    both = []
    for st in range(EARLY):
        lo = st * C64
        z_copies[st].wait_recv()
        z_copies[EARLY + st].wait_recv()
        scale = jnp.concatenate([cc[k][:, lo : lo + C64] * coef[k] for k in range(2)], axis=1)
        step_part = acc[EARLY + st, 0:B, :] + zin_v[st].astype(jnp.float32)
        both.append(acc[st, 0:B, :] + zbuf[st] - step_part * scale)
    finish(0, both[0], both[1])
    for stage, slot in enumerate((dp1, rx, tx, rz, tz, dp2)):
        sent(slot, stage)
    for c in tok_out + z_copies[: 2 * EARLY]:
        c.wait_send()

    def left(st):
        for way in range(2):
            for t in range(1, steps(way, st) + 1):
                for h in range(pieces(st)):
                    ag_copy(way, st, t, h).wait_send()

    for st in range(2 * EARLY):
        left(st)

    both = []
    for st in late:
        relay(st, 4)
        i = st - 2 * EARLY
        part = jnp.dot(tokbuf[across, 0:B, :], agbuf[st, across], preferred_element_type=jnp.float32)
        z_copies[st].wait_recv()
        part += acc[st, 0:B, :] + zin_v[st - EARLY].astype(jnp.float32)
        for h in range(pieces(st)):
            far_copy(far_way(st), st, h).wait_recv()
        both.append(part + jnp.dot(tok_far[...], xbuf[i], preferred_element_type=jnp.float32))
    finish(1, both[0], both[1])

    for st in late:
        left(st)
        z_copies[st].wait_send()
        for h in range(pieces(st)):
            far_copy(far_way(st), st, h).wait_send()


def copy_kernel(*refs):
    sems = refs[-1]
    n = (len(refs) - 1) // 2
    copies = [pltpu.make_async_copy(refs[i], refs[n + i], sems.at[i]) for i in range(n)]
    for c in copies:
        c.start()
    for c in copies:
        c.wait()


def per_device(tokens, iw, ig, irow, icol, ow, og, orow, ocol):
    f32, bf16 = jnp.float32, jnp.bfloat16
    hbm = pl.BlockSpec(memory_space=pl.ANY)
    vm = pl.BlockSpec(memory_space=pltpu.VMEM)
    sds = jax.ShapeDtypeStruct
    shapes = (
        sds((2, B, B), f32), sds((2, B, B), f32), sds((2, B), f32), sds((2, B), f32),
        sds((B, B), f32), sds((B, B), f32), sds((1, B), f32), sds((1, B), f32), sds((B, B), bf16),
    )
    dma = pltpu.SemaphoreType.DMA
    outs = pl.pallas_call(
        kernel,
        out_shape=tuple(pltpu.VMEM(a.shape, a.dtype) for a in shapes),
        in_specs=[hbm, hbm, hbm, vm, vm, hbm, hbm, vm, vm],
        out_specs=(vm,) * len(shapes),
        scratch_shapes=[
            pltpu.VMEM((3, B, B), f32),
            pltpu.VMEM((3, B, B), f32),
            pltpu.VMEM((3, B, B), f32),
            pltpu.VMEM((CHUNKS - EARLY, B, H), f32),
            pltpu.VMEM((CHUNKS - EARLY, B, H), f32),
            pltpu.VMEM((NY, 2 * B, B), bf16),
            pltpu.VMEM((B, B), bf16),
            pltpu.VMEM((CHUNKS - EARLY, B, H), bf16),
            pltpu.VMEM((STREAMS, NY, B, H), bf16),
            pltpu.VMEM((STREAMS, 2 * B, H), f32),
            pltpu.VMEM((EARLY, B, H), f32),
            pltpu.VMEM((CHUNKS, B, H), bf16),
            pltpu.VMEM((CHUNKS, B, H), bf16),
            pltpu.VMEM((16, 8, H), f32),
            pltpu.VMEM((8, 8, H), f32),
            pltpu.VMEM((8, 8, H), f32),
            pltpu.VMEM((8, 8, H), f32),
            pltpu.VMEM((8, 8, H), f32),
            pltpu.VMEM((16, 8, H), f32),
            pltpu.VMEM((6, 8, H), f32),
            pltpu.VMEM((24, H), f32),
            pltpu.VMEM((H, H), f32),
            dma((4,)), dma((NY + 1,)), dma((6,)), dma((6,)), dma((4,)), dma((4,)), dma((4,)), dma((4,)),
            dma((2, STREAMS, 4, 2)), dma((2, STREAMS, 4, 2)), dma((CHUNKS - EARLY, 2)), dma((CHUNKS - EARLY, 2)), dma((STREAMS,)), dma((STREAMS,)),
        ],
        compiler_params=pltpu.CompilerParams(
            collective_id=0, has_side_effects=True, vmem_limit_bytes=61 * 1024 * 1024
        ),
        cost_estimate=pl.CostEstimate(
            flops=2 * B * D * 2 * B, bytes_accessed=5 * 1024 * 1024, transcendentals=B * B
        ),
    )(tokens, iw, ig, irow, icol, ow, og, orow.reshape(1, B), ocol.reshape(1, B))
    outs = pl.pallas_call(
        copy_kernel,
        out_shape=shapes,
        in_specs=[vm] * len(shapes),
        out_specs=(hbm,) * len(shapes),
        scratch_shapes=[dma((len(shapes),))],
    )(*[pltpu.with_memory_space_constraint(o, pltpu.VMEM) for o in outs])
    outs = list(outs)
    outs[6] = outs[6].reshape(B)
    outs[7] = outs[7].reshape(B)
    return tuple(outs)


def solution(mesh):
    placed = (
        P("dp", None),
        P(None, "dp", "mp"),
        P(None, "dp", "mp"),
        P(None, "dp"),
        P(None, "mp"),
        P("mp", "dp"),
        P("mp", "dp"),
        P("mp"),
        P("dp"),
    )
    return jax.shard_map(
        per_device,
        mesh=mesh,
        in_specs=placed,
        out_specs=(
            P(None, "dp", "mp"),
            P(None, "dp", "mp"),
            P(None, "dp"),
            P(None, "mp"),
            P("mp", "dp"),
            P("mp", "dp"),
            P("mp"),
            P("dp"),
            P("dp", "mp"),
        ),
        check_vma=False,
    )
```

```python
import functools

import jax
import jax.numpy as jnp
from jax import lax
from jax.experimental import pallas as pl
from jax.experimental.pallas import tpu as pltpu
from jax.sharding import PartitionSpec as P

D = 4096
FF = 16384
STEP = 10
FORGET = 1.0 - STEP ** (-0.8)
FRESH = 1.0 - FORGET
RELATIVE = min(0.01, STEP ** (-0.5))

NY = 8
B = 256
H = 128
CHUNKS = 4
EARLY = 2
STREAMS = 2 * EARLY + CHUNKS - EARLY
C64 = 64
MESH = pl.DeviceIdType.MESH


def rows_to_lanes(q):
    return jnp.sum((q[:, :H] + q[:, H:]).T, axis=0, keepdims=True)


def lanes_to_rows(v):
    return jnp.concatenate(
        [jnp.broadcast_to(v[:, :H], (H, H)).T, jnp.broadcast_to(v[:, H:], (H, H)).T], axis=0
    )


def far_first(n):
    return sorted(range(1, n), key=lambda k: -min(k, n - k))


def kernel(
    tok, iw, ig, irow, icol, ow, og, orow, ocol,
    inew, iupd, irow_new, icol_new, onew, oupd, orow_new, ocol_new, hid,
    g_v, w_v, raw, late_w, late_raw, tokbuf, tok_far, xbuf, agbuf, acc, zbuf, zout_v, zin_v,
    dp1, rx, rz, tx, tz, dp2, snd, scal, rmat,
    load_sem, tok_sem, st_send, st_recv, tx_send, tx_recv, sib_send, sib_recv,
    ag_send, ag_recv, x_send, x_recv, z_send, z_recv,
):
    dp, mp = lax.axis_index("dp"), lax.axis_index("mp")
    y, z = dp // 2, lax.rem(dp, 2)
    x, zc = mp // 8, lax.rem(mp, 8)
    core = lax.rem(mp, 2)

    dp_peers = [(lax.rem(dp + k, 16), mp) for k in far_first(16)]
    x_peers = [(dp, lax.rem(x + k, 8) * 8 + zc) for k in far_first(8)]
    zc_peers = [(dp, x * 8 + lax.rem(zc + k, 8)) for k in far_first(8)]
    y_next = (lax.rem(y + 1, NY) * 2 + z, mp)
    y_prev = (lax.rem(y + NY - 1, NY) * 2 + z, mp)
    z_pair = (y * 2 + 1 - z, mp)
    y_next_pair = (lax.rem(y + 1, NY) * 2 + 1 - z, mp)
    y_prev_pair = (lax.rem(y + NY - 1, NY) * 2 + 1 - z, mp)
    across = lax.rem(y + 4, NY)
    sibling = (dp, mp + 1 - 2 * core)

    loads = [
        pltpu.make_async_copy(ig, g_v.at[pl.ds(0, 2)], load_sem.at[0]),
        pltpu.make_async_copy(og, g_v.at[2], load_sem.at[1]),
        pltpu.make_async_copy(iw, w_v.at[pl.ds(0, 2)], load_sem.at[2]),
        pltpu.make_async_copy(ow, w_v.at[2], load_sem.at[3]),
    ]
    for c in loads:
        c.start()

    barrier = pltpu.get_barrier_semaphore()
    for peer in dp_peers + x_peers + zc_peers:
        pl.semaphore_signal(barrier, inc=1, device_id=peer, device_id_type=MESH)

    def put(i, row, v):
        snd[i, row : row + 1, :] = v[:, :H]
        snd[i, row + 1 : row + 2, :] = v[:, H:]

    def take(row):
        return jnp.concatenate([scal[row : row + 1, :], scal[row + 1 : row + 2, :]], axis=1)

    def exchange(slot, me, peers, src, stage):
        for p in peers:
            pltpu.make_async_remote_copy(
                src_ref=src, dst_ref=slot.at[me], send_sem=st_send.at[stage], recv_sem=st_recv.at[stage],
                device_id=p, device_id_type=MESH,
            ).start()
        slot[me] = src[...]

    def arrived(slot, stage):
        n = slot.shape[0]
        part = slot.at[pl.ds(0, n - 1)]
        pltpu.make_async_copy(part, part, st_recv.at[stage]).wait()
        tot = slot[0]
        for i in range(1, n):
            tot = tot + slot[i]
        return tot

    def sent(slot, stage):
        part = slot.at[pl.ds(0, slot.shape[0] - 1)]
        pltpu.make_async_copy(part, part, st_send.at[stage]).wait()

    def ag_copy(way, st, s, h):
        src = lax.rem(y + NY - (s - 1), NY) if way == 0 else lax.rem(y + s - 1, NY)
        rows = B // pieces(st)
        part = agbuf.at[st, src, pl.ds(h * rows, rows), :]
        return pltpu.make_async_remote_copy(
            src_ref=part, dst_ref=part,
            send_sem=ag_send.at[way, st, s - 1, h], recv_sem=ag_recv.at[way, st, s - 1, h],
            device_id=y_next if way == 0 else y_prev, device_id_type=MESH,
        )

    def pieces(st):
        return 1 if st < 2 * EARLY else 2

    def steps(way, st):
        return 4 if (st % 2 == 0) == (way == 0) else 3

    def origin(way, s):
        return lax.rem(y + NY - s, NY) if way == 0 else lax.rem(y + s, NY)

    def pack(pair, c):
        lo = c * C64
        return jnp.concatenate([pair[0, :, lo : lo + C64], pair[1, :, lo : lo + C64]], axis=1)

    def launch(st, block):
        agbuf[st, y] = block.astype(jnp.bfloat16)
        for h in range(pieces(st)):
            for way in range(2):
                ag_copy(way, st, 1, h).start()

    def far_copy(way, st, h):
        rows = B // pieces(st)
        src = lax.rem(y + NY - 3, NY) if way == 0 else lax.rem(y + 3, NY)
        return pltpu.make_async_remote_copy(
            src_ref=agbuf.at[st, src, pl.ds(h * rows, rows), :],
            dst_ref=xbuf.at[st - 2 * EARLY, pl.ds(h * rows, rows), :],
            send_sem=x_send.at[st - 2 * EARLY, h], recv_sem=x_recv.at[st - 2 * EARLY, h],
            device_id=y_next_pair if way == 0 else y_prev_pair, device_id_type=MESH,
        )

    def far_way(st):
        return 0 if steps(0, st) == 4 else 1

    def relay(st, s):
        for h in range(pieces(st)):
            for way in range(2):
                if s <= steps(way, st):
                    ag_copy(way, st, s, h).wait_recv()
                    if s < steps(way, st):
                        ag_copy(way, st, s + 1, h).start()
                        if s == 3 and st >= 2 * EARLY:
                            far_copy(way, st, h).start()

    def product(st, b, first=False):
        part = jnp.dot(tokbuf[b], agbuf[st, b], preferred_element_type=jnp.float32)
        if first:
            acc[st] = part
        else:
            acc[st] += part

    def products(st, s):
        for way in range(2):
            if s <= steps(way, st):
                product(st, origin(way, s))

    snd[...] = jnp.zeros_like(snd)
    loads[0].wait()
    for k in range(2):
        g = g_v[k]
        put(0, 2 * k, jnp.sum(g * g + 1e-30, axis=0, keepdims=True))
    loads[1].wait()
    g = g_v[2]
    put(0, 4, rows_to_lanes(g * g + 1e-30))

    pl.semaphore_wait(barrier, 29)
    exchange(dp1, dp, dp_peers, snd.at[0], 0)

    loads[2].wait()
    for c in range(EARLY):
        launch(c, pack(w_v, c))
    for c in range(EARLY):
        launch(EARLY + c, pack(g_v, c))
    own_tok = [
        pltpu.make_async_copy(
            tok.at[:, pl.ds(pl.multiple_of((2 * across + 1 - z) * B, B), B)], tok_far, tok_sem.at[NY]
        )
    ]
    own_tok[0].start()
    for b in range(NY):
        c = pltpu.make_async_copy(
            tok.at[:, pl.ds(pl.multiple_of((2 * b + z) * B, B), B)],
            tokbuf.at[b, pl.ds(0, B), :],
            tok_sem.at[b],
        )
        c.start()
        own_tok.append(c)

    tok_out = []
    for j in range(4):
        b = core * 4 + j
        c = pltpu.make_async_remote_copy(
            src_ref=tok.at[:, pl.ds(pl.multiple_of((2 * b + 1 - z) * B, B), B)],
            dst_ref=tokbuf.at[b, pl.ds(B, B), :],
            send_sem=tx_send.at[j], recv_sem=tx_recv.at[j],
            device_id=z_pair, device_id_type=MESH,
        )
        c.start()
        tok_out.append(c)

    for k in range(2):
        g = g_v[k]
        put(1, 2 * k, rows_to_lanes(g * g + 1e-30))
    g = g_v[2]
    put(1, 4, jnp.sum(g * g + 1e-30, axis=0, keepdims=True))
    exchange(rx, x, x_peers, snd.at[1], 1)
    loads[3].wait()
    lane1 = lax.broadcasted_iota(jnp.int32, (1, H), 1)
    misc = jnp.zeros((1, H), jnp.float32)
    for k in range(3):
        w = w_v[k]
        v = jnp.sum(w * w, axis=0, keepdims=True)
        misc = jnp.where(lane1 == k, jnp.sum(v, axis=1, keepdims=True), misc)

    scal[0:8, :] = arrived(dp1, 0)
    old = [icol[0:1, :], icol[1:2, :], orow[...]]
    fc = [FORGET * old[k] + FRESH * (take(2 * k) / D) for k in range(3)]
    cc = [lax.rsqrt(f) for f in fc]
    misc = jnp.where(lane1 == 3, jnp.sum(fc[2], axis=1, keepdims=True), misc)
    snd[2, 6:7, :] = misc
    for k in range(2):
        g = g_v[k] * cc[k]
        raw[k] = g
        put(2, 2 * k, rows_to_lanes(g * g))
    c2 = lanes_to_rows(cc[2])
    g = g_v[2] * jnp.concatenate([c2, c2], axis=1)
    raw[2] = g
    put(2, 4, jnp.sum(g * g, axis=0, keepdims=True))
    exchange(tx, x, x_peers, snd.at[2], 2)
    icol_new[0:1, :] = fc[0]
    icol_new[1:2, :] = fc[1]
    orow_new[...] = fc[2]

    relay(0, 1)
    relay(1, 1)
    snd[3] = arrived(rx, 1)
    exchange(rz, zc, zc_peers, snd.at[3], 3)
    relay(2, 1)
    relay(3, 1)
    snd[4] = arrived(tx, 2)
    exchange(tz, zc, zc_peers, snd.at[4], 4)
    for st in range(2 * EARLY):
        relay(st, 2)
    sib_out = []
    for j in range(4):
        b = core * 4 + j
        tok_out[j].wait_recv()
        c = pltpu.make_async_remote_copy(
            src_ref=tokbuf.at[b, pl.ds(B, B), :],
            dst_ref=tokbuf.at[b, pl.ds(B, B), :],
            send_sem=sib_send.at[j], recv_sem=sib_recv.at[j],
            device_id=sibling, device_id_type=MESH,
        )
        c.start()
        sib_out.append(c)
    for t in (3, 4):
        for st in range(2 * EARLY):
            relay(st, t)

    for c in own_tok:
        c.wait()
    for c in sib_out:
        c.wait()
    for st in range(EARLY):
        product(st, y, True)
        for t in range(1, 4):
            products(st, t)
    z_copies = []
    for st in range(EARLY):
        products(st, 4)
        c = pltpu.make_async_remote_copy(
            src_ref=acc.at[st, pl.ds(B, B), :], dst_ref=zbuf.at[st],
            send_sem=z_send.at[st], recv_sem=z_recv.at[st], device_id=z_pair, device_id_type=MESH,
        )
        c.start()
        z_copies.append(c)

    scal[8:16, :] = arrived(rz, 3)
    scal[16:24, :] = arrived(tz, 4)
    old = [irow[0:1, :], irow[1:2, :], ocol[...]]
    fr = []
    for k in range(3):
        f = FORGET * old[k] + FRESH * (take(8 + 2 * k) / FF)
        fr.append(f)
        u = take(16 + 2 * k) / f
        snd[5, k : k + 1, :] = u[:, :H] + u[:, H:]
    snd[5, 3:4, :] = scal[22:23, :]
    put(5, 4, fr[0])
    put(5, 6, fr[1])
    exchange(dp2, dp, dp_peers, snd.at[5], 5)
    irow_new[0:1, :] = fr[0]
    irow_new[1:2, :] = fr[1]
    ocol_new[...] = fr[2]
    mean2 = scal[22:23, 3:4] / FF

    for k in range(2):
        rr = lanes_to_rows(lax.rsqrt(fr[k]))
        raw[k] = raw[k] * jnp.concatenate([rr, rr], axis=1)
    raw[2] = raw[2] * lax.rsqrt(fr[2])

    late = range(2 * EARLY, STREAMS)
    for st in late:
        late_w[st - 2 * EARLY] = pack(w_v, st - EARLY)
        late_raw[st - 2 * EARLY] = pack(raw, st - EARLY)
    scal[0:8, :] = arrived(dp2, 5)
    s = [jnp.sum(scal[k : k + 1, :], axis=1, keepdims=True) for k in range(3)]
    mean = [jnp.sum(take(4 + 2 * k), axis=1, keepdims=True) / D for k in range(2)] + [mean2]
    coef = []
    for k in range(3):
        clip = jnp.maximum(1.0, jnp.sqrt(s[k] * mean[k] / (D * FF)))
        step = RELATIVE * jnp.sqrt(scal[3:4, k : k + 1] / (D * FF))
        coef.append(step / clip * jnp.sqrt(mean[k]))

    both_coef = jnp.where(lane1 < C64, coef[0], coef[1])
    for st in late:
        i = st - 2 * EARLY
        launch(st, late_w[i] + late_raw[i] * (-both_coef))
    for k in range(2):
        u = raw[k] * (-coef[k])
        iupd[k] = u
        inew[k] = w_v[k] + u

    def z_exchange(st):
        i = st - EARLY
        zout_v[i] = acc[st, B : 2 * B, :].astype(jnp.bfloat16)
        c = pltpu.make_async_remote_copy(
            src_ref=zout_v.at[i], dst_ref=zin_v.at[i],
            send_sem=z_send.at[st], recv_sem=z_recv.at[st], device_id=z_pair, device_id_type=MESH,
        )
        c.start()
        z_copies.append(c)

    u = raw[2] * (-coef[2])
    oupd[...] = u
    onew[...] = w_v[2] + u

    rmat[...] = jnp.ones((H, H), jnp.float32)
    for b in range(NY):
        rmat[4 * b : 4 * b + 4, :] = lax.rsqrt(dp2[2 * b + z, 4:8, :])
    rmat[...] = rmat[...].T
    low = lax.broadcasted_iota(jnp.int32, (H, H), 1) < C64

    def scaled_products(b):
        halves = []
        for h in range(2):
            j = 4 * b + h
            halves.append(
                jnp.where(
                    low,
                    jnp.broadcast_to(rmat[:, j : j + 1], (H, H)),
                    jnp.broadcast_to(rmat[:, j + 2 : j + 3], (H, H)),
                )
            )
        rr = jnp.concatenate(halves, axis=0)
        for st in range(EARLY, 2 * EARLY):
            rows = (agbuf[st, b].astype(jnp.float32) * rr).astype(jnp.bfloat16)
            part = jnp.dot(tokbuf[b], rows, preferred_element_type=jnp.float32)
            if b == 0:
                acc[st] = part
            else:
                acc[st] += part

    for b in range(0, 3):
        scaled_products(b)
    for st in late:
        relay(st, 1)
    for b in range(3, 6):
        scaled_products(b)
    for st in late:
        relay(st, 2)
    for b in range(6, NY):
        scaled_products(b)
    for st in range(EARLY, 2 * EARLY):
        z_exchange(st)
    for st in late:
        product(st, y, True)
        products(st, 1)
        products(st, 2)
    for st in late:
        relay(st, 3)
    for st in late:
        products(st, 3)
        z_exchange(st)

    lane = lax.broadcasted_iota(jnp.int32, (B, H), 1)

    def finish(p, left, right):
        gate = jnp.where(lane < C64, left, pltpu.roll(right, C64, 1))
        up = jnp.where(lane < C64, pltpu.roll(left, C64, 1), right)
        hid[:, p * H : (p + 1) * H] = (jax.nn.gelu(gate, approximate=True) * up).astype(jnp.bfloat16)

    both = []
    for st in range(EARLY):
        lo = st * C64
        z_copies[st].wait_recv()
        z_copies[EARLY + st].wait_recv()
        scale = jnp.concatenate([cc[k][:, lo : lo + C64] * coef[k] for k in range(2)], axis=1)
        step_part = acc[EARLY + st, 0:B, :] + zin_v[st].astype(jnp.float32)
        both.append(acc[st, 0:B, :] + zbuf[st] - step_part * scale)
    finish(0, both[0], both[1])
    for stage, slot in enumerate((dp1, rx, tx, rz, tz, dp2)):
        sent(slot, stage)
    for c in tok_out + z_copies[: 2 * EARLY]:
        c.wait_send()

    def left(st):
        for way in range(2):
            for t in range(1, steps(way, st) + 1):
                for h in range(pieces(st)):
                    ag_copy(way, st, t, h).wait_send()

    for st in range(2 * EARLY):
        left(st)

    both = []
    for st in late:
        relay(st, 4)
        i = st - 2 * EARLY
        part = jnp.dot(tokbuf[across, 0:B, :], agbuf[st, across], preferred_element_type=jnp.float32)
        z_copies[st].wait_recv()
        part += acc[st, 0:B, :] + zin_v[st - EARLY].astype(jnp.float32)
        for h in range(pieces(st)):
            far_copy(far_way(st), st, h).wait_recv()
        both.append(part + jnp.dot(tok_far[...], xbuf[i], preferred_element_type=jnp.float32))
    finish(1, both[0], both[1])

    for st in late:
        left(st)
        z_copies[st].wait_send()
        for h in range(pieces(st)):
            far_copy(far_way(st), st, h).wait_send()


def copy_kernel(*refs):
    sems = refs[-1]
    n = (len(refs) - 1) // 2
    copies = [pltpu.make_async_copy(refs[i], refs[n + i], sems.at[i]) for i in range(n)]
    for c in copies:
        c.start()
    for c in copies:
        c.wait()


def per_device(tokens, iw, ig, irow, icol, ow, og, orow, ocol):
    f32, bf16 = jnp.float32, jnp.bfloat16
    hbm = pl.BlockSpec(memory_space=pl.ANY)
    vm = pl.BlockSpec(memory_space=pltpu.VMEM)
    sds = jax.ShapeDtypeStruct
    shapes = (
        sds((2, B, B), f32), sds((2, B, B), f32), sds((2, B), f32), sds((2, B), f32),
        sds((B, B), f32), sds((B, B), f32), sds((1, B), f32), sds((1, B), f32), sds((B, B), bf16),
    )
    dma = pltpu.SemaphoreType.DMA
    outs = pl.pallas_call(
        kernel,
        out_shape=tuple(pltpu.VMEM(a.shape, a.dtype) for a in shapes),
        in_specs=[hbm, hbm, hbm, vm, vm, hbm, hbm, vm, vm],
        out_specs=(vm,) * len(shapes),
        scratch_shapes=[
            pltpu.VMEM((3, B, B), f32),
            pltpu.VMEM((3, B, B), f32),
            pltpu.VMEM((3, B, B), f32),
            pltpu.VMEM((CHUNKS - EARLY, B, H), f32),
            pltpu.VMEM((CHUNKS - EARLY, B, H), f32),
            pltpu.VMEM((NY, 2 * B, B), bf16),
            pltpu.VMEM((B, B), bf16),
            pltpu.VMEM((CHUNKS - EARLY, B, H), bf16),
            pltpu.VMEM((STREAMS, NY, B, H), bf16),
            pltpu.VMEM((STREAMS, 2 * B, H), f32),
            pltpu.VMEM((EARLY, B, H), f32),
            pltpu.VMEM((CHUNKS, B, H), bf16),
            pltpu.VMEM((CHUNKS, B, H), bf16),
            pltpu.VMEM((16, 8, H), f32),
            pltpu.VMEM((8, 8, H), f32),
            pltpu.VMEM((8, 8, H), f32),
            pltpu.VMEM((8, 8, H), f32),
            pltpu.VMEM((8, 8, H), f32),
            pltpu.VMEM((16, 8, H), f32),
            pltpu.VMEM((6, 8, H), f32),
            pltpu.VMEM((24, H), f32),
            pltpu.VMEM((H, H), f32),
            dma((4,)), dma((NY + 1,)), dma((6,)), dma((6,)), dma((4,)), dma((4,)), dma((4,)), dma((4,)),
            dma((2, STREAMS, 4, 2)), dma((2, STREAMS, 4, 2)), dma((CHUNKS - EARLY, 2)), dma((CHUNKS - EARLY, 2)), dma((STREAMS,)), dma((STREAMS,)),
        ],
        compiler_params=pltpu.CompilerParams(
            collective_id=0, has_side_effects=True, vmem_limit_bytes=61 * 1024 * 1024
        ),
        cost_estimate=pl.CostEstimate(
            flops=2 * B * D * 2 * B, bytes_accessed=5 * 1024 * 1024, transcendentals=B * B
        ),
    )(tokens, iw, ig, irow, icol, ow, og, orow.reshape(1, B), ocol.reshape(1, B))
    outs = pl.pallas_call(
        copy_kernel,
        out_shape=shapes,
        in_specs=[vm] * len(shapes),
        out_specs=(hbm,) * len(shapes),
        scratch_shapes=[dma((len(shapes),))],
    )(*[pltpu.with_memory_space_constraint(o, pltpu.VMEM) for o in outs])
    outs = list(outs)
    outs[6] = outs[6].reshape(B)
    outs[7] = outs[7].reshape(B)
    return tuple(outs)


def solution(mesh):
    placed = (
        P("dp", None),
        P(None, "dp", "mp"),
        P(None, "dp", "mp"),
        P(None, "dp"),
        P(None, "mp"),
        P("mp", "dp"),
        P("mp", "dp"),
        P("mp"),
        P("dp"),
    )
    return jax.shard_map(
        per_device,
        mesh=mesh,
        in_specs=placed,
        out_specs=(
            P(None, "dp", "mp"),
            P(None, "dp", "mp"),
            P(None, "dp"),
            P(None, "mp"),
            P("mp", "dp"),
            P("mp", "dp"),
            P("mp"),
            P("dp"),
            P("dp", "mp"),
        ),
        check_vma=False,
    )
```
